32 devices in a mesh: pair: 8 (over y, x, core), sec: 4 (over z).
Axes of the slice: x: 2, y: 2, z: 4, core: 2. Of those that a mesh axis runs over, the one named last changes fastest.
Arguments:
- normal_ops: float32 [2, 16, 128, 512], P(None, 'pair', None, 'sec'), may hold values from -6 to 6
- integrals: float32 [2, 8, 16], P(None, 'pair'), may hold values from -2 to 2
- site_terms: float32 [2, 8, 4, 4], P(None, 'pair'), may hold values from -8 to 8
- basis: float32 [2, 4, 512, 512], P(None, None, None, 'sec'), may hold values from -0.25 to 0.25
Outputs:
- new_normal: float32 [2, 16, 4, 128, 512], P(None, 'pair', None, None, 'sec')
- new_comp: float32 [2, 8, 4, 128, 512], P(None, 'pair', None, None, 'sec')
The draws below stay inside these ranges and needn't reach their ends.
All inputs are finite; a program needn't handle non-finite values.
Results may differ from the reference program's by a relative error of at most 0.00007.
Values sent between devices are 32-bit elements; how exact they have to be, the bound alone decides.
No kernel may reach another device: no remote copies, remote signals or barrier semaphores. Data moves between devices by JAX's collectives and lax.ppermute only.
A program may use at most 64 MiB of HBM per device.

```python
import jax
import jax.numpy as jnp
from jax import lax

SDIM = 512
SITE = 4
ROWS = 128
NORM = 16
COMP = 8


def strengthened(drawn, rng, source, target, blocks, factor):
    owner, partner = [(jnp.arange(drawn.shape[position]) // (drawn.shape[position] // blocks)).reshape([-1 if axis == position else 1 for axis in range(drawn.ndim)]) for position in (source, target)]
    chosen = jax.random.permutation(rng, blocks)[partner]
    strong = (owner == chosen) | (owner == (partner + blocks // 2) % blocks)
    return jnp.where(strong, factor * drawn, drawn)


def block_levels(rng, extent, shards, least, largest):
    def one(axis_at, parts):
        heights = jax.random.uniform(jax.random.fold_in(jax.random.fold_in(rng, 6), axis_at), (parts,), jnp.float32, least / len(shards), largest / len(shards))
        return jnp.repeat(jnp.exp(heights), extent[axis_at] // parts).reshape((-1,) + (1,) * (len(extent) - axis_at - 1))

    loudness = one(*shards[0])
    for cut in shards[1:]:
        loudness = loudness * one(*cut)
    return loudness


def scatter_about(stream_key, shape, spread, limit, pieces=(), held_as=jnp.bfloat16):
    values = spread * jax.random.normal(stream_key, shape, jnp.float32)
    if pieces:
        values = values * block_levels(stream_key, shape, pieces, -0.22, 0.18)
    return jnp.clip(values, -limit, limit).astype(held_as)


def heavy_noise(key, dims, scale, most, pieces, heavy, kind=jnp.bfloat16):
    array = scale * jax.random.normal(key, dims, jnp.float32)
    if pieces:
        array = array * block_levels(key, dims, pieces, -0.22, 0.18)
    return jnp.clip(strengthened(array, jax.random.fold_in(key, 3), *heavy), -most, most).astype(kind)


def setup_inputs(seed: int = 0) -> dict:
    arg_keys = jax.random.split(jax.random.key(seed), 5)
    normal_ops = scatter_about(arg_keys[0], (2, NORM, ROWS, SDIM), 1.0, 6.0, ((1, 8), (3, 4)), jnp.float32)
    integrals = heavy_noise(arg_keys[1], (2, COMP, NORM), NORM ** -0.5, 2.0, ((1, 8),), (2, 1, 8, 2.0), jnp.float32)
    site_terms = scatter_about(arg_keys[2], (2, COMP, SITE, SITE), 2.0, 8.0, ((1, 8),), jnp.float32)
    basis = scatter_about(arg_keys[3], (2, SITE, SDIM, SDIM), SDIM ** -0.5, 0.25, ((3, 4),), jnp.float32)
    return {"normal_ops": normal_ops, "integrals": integrals, "site_terms": site_terms, "basis": basis}


highest = lax.Precision.HIGHEST


def complex_einsum(form, left, right):
    real_part = jnp.einsum(form, left[0], right[0], precision=highest) - jnp.einsum(form, left[1], right[1], precision=highest)
    imag_part = jnp.einsum(form, left[0], right[1], precision=highest) + jnp.einsum(form, left[1], right[0], precision=highest)
    return jnp.stack([real_part, imag_part])


def reference(normal_ops, integrals, site_terms, basis):
    comp_ops = complex_einsum("pr,rxc->pxc", integrals, normal_ops)
    row_count = normal_ops.shape[2]

    def renorm_one(operator):
        return complex_einsum("ij,ajn->ain", operator, basis)

    new_normal = lax.map(renorm_one, jnp.transpose(normal_ops, (1, 0, 2, 3)))
    new_normal = jnp.transpose(new_normal, (1, 0, 2, 3, 4))
    new_comp = lax.map(renorm_one, jnp.transpose(comp_ops, (1, 0, 2, 3)))
    new_comp = jnp.transpose(new_comp, (1, 0, 2, 3, 4))
    site_part = complex_einsum("pab,bin->pain", site_terms, basis[:, :, :row_count, :])
    return new_normal, new_comp + site_part
```

```python
import functools

import jax
import jax.numpy as jnp
from jax import lax
from jax.experimental import pallas as pl
from jax.experimental.pallas import tpu as pltpu
from jax.sharding import PartitionSpec as P

VMEM_BYTES = 24 * 1024 * 1024
WIDE = 256
TILE = (8, 128)
VMEM = pl.BlockSpec(memory_space=pltpu.VMEM)
ANY = pl.BlockSpec(memory_space=pl.ANY)
HBM = pl.BlockSpec(memory_space=pltpu.HBM)


def call(kernel, out_shape, in_specs, flops, scratch_shapes=()):
    return pl.pallas_call(
        kernel,
        out_shape=out_shape,
        in_specs=in_specs,
        out_specs=jax.tree.map(lambda _: VMEM, out_shape),
        scratch_shapes=scratch_shapes,
        cost_estimate=pl.CostEstimate(flops=flops, bytes_accessed=4 << 20, transcendentals=0),
        compiler_params=pltpu.CompilerParams(vmem_limit_bytes=VMEM_BYTES),
    )


def split(x):
    high = x.astype(jnp.bfloat16)
    return high, (x - high.astype(jnp.float32)).astype(jnp.bfloat16)


def order(sec):
    return (1, 0) + tuple(range(2, sec))


def prepare_kernel(depth, basis_hbm, site_hbm, high_ref, low_ref, part_ref, *scratch):
    basis_ref, site_ref, basis_sem, site_sem = scratch
    _, sites, old, cols = basis_ref.shape
    rows = part_ref.shape[3]
    me = lax.axis_index("sec")
    site_copy = pltpu.make_async_copy(site_hbm, site_ref, site_sem)
    site_copy.start()
    copies = [
        (part, site, pltpu.make_async_copy(
            basis_hbm.at[part, site], basis_ref.at[part, site], basis_sem.at[part, site]
        ))
        for part in range(2)
        for site in range(sites)
    ]
    for _, _, copy in copies:
        copy.start()
    for part, site, copy in copies:
        copy.wait()
        for step, far in enumerate(order(old // depth)):
            start = pl.multiple_of((me ^ far) * depth, depth)
            at = pl.ds((step * 2 + part) * depth, depth)
            high, low = split(basis_ref[part, site, pl.ds(start, depth), :])
            high_ref[at, pl.ds(site * cols, cols)] = high
            low_ref[at, pl.ds(site * cols, cols)] = low
    site_copy.wait()
    for comp in range(part_ref.shape[1]):
        for site in range(sites):
            real = imag = None
            for other in range(sites):
                sr, si = site_ref[0, comp, site, other], site_ref[1, comp, site, other]
                br, bi = basis_ref[0, other, :rows, :], basis_ref[1, other, :rows, :]
                tr, ti = sr * br - si * bi, sr * bi + si * br
                real = tr if real is None else real + tr
                imag = ti if imag is None else imag + ti
            part_ref[0, comp, site] = real
            part_ref[1, comp, site] = imag


def prepare(basis, site_terms, rows, depth):
    _, sites, old, cols = basis.shape
    comps = site_terms.shape[1]
    half = jax.ShapeDtypeStruct((2 * old, sites * cols), jnp.bfloat16)
    part = jax.ShapeDtypeStruct((2, comps, sites, rows, cols), jnp.float32)
    return call(
        functools.partial(prepare_kernel, depth),
        (half, half, part),
        [HBM, HBM],
        8 * comps * sites * sites * rows * cols,
        [
            pltpu.VMEM(basis.shape, basis.dtype),
            pltpu.SMEM(site_terms.shape, site_terms.dtype),
            pltpu.SemaphoreType.DMA((2, sites)),
            pltpu.SemaphoreType.DMA,
        ],
    )(basis, site_terms)


def tile(integrals):
    _, comps, norms = integrals.shape

    def kernel(integrals_ref, out_ref):
        out_ref[...] = jnp.zeros(TILE, jnp.float32)
        for part in range(2):
            out_ref[part * comps : (part + 1) * comps, :norms] = integrals_ref[part]

    return call(kernel, jax.ShapeDtypeStruct(TILE, jnp.float32), [VMEM], 0)(integrals)


def pack(block, ops, tiles):
    _, _, rows, cols = block.shape

    def kernel(block_ref, *refs):
        out_ref = refs[-1]
        out_ref[:, :, :rows, :] = block_ref[:, ops.start : ops.stop]
        out_ref[:, :, rows:, :] = jnp.zeros((2, len(ops)) + TILE, jnp.float32)
        for part, ref in enumerate(refs[:-1]):
            out_ref[part, 0, rows:, :] = ref[...]

    out = jax.ShapeDtypeStruct((2, len(ops), rows + TILE[0], cols), block.dtype)
    return call(kernel, out, [VMEM] * (1 + len(tiles)), 0)(block, *tiles)


def after(x, *others):
    def kernel(x_ref, *refs):
        refs[-1][...] = x_ref[...]

    out = jax.ShapeDtypeStruct(x.shape, x.dtype)
    return call(kernel, out, [VMEM] + [ANY] * len(others), 0)(x, *others)


def renorm_kernel(steps, parts, carried, *refs):
    count = sum(parts)
    high_ref, low_ref = refs[count : count + 2]
    out_ref, token_ref, left_high, left_low = refs[-4:]
    token_ref[...] = jnp.zeros(TILE, jnp.float32)
    _, ops, sites, rows, cols = out_ref.shape
    depth = refs[0].shape[-1]
    tall = ops * rows
    for step in range(len(steps)):
        first = sum(parts[:step])
        value = sum(refs[at][:, :, :rows, :] for at in range(first + 1, first + parts[step]))
        value = (refs[first][:, :, :rows, :] + value).reshape(2, tall, depth)
        for scratch, real, imag in zip((left_high, left_low), split(value[0]), split(value[1])):
            at = 2 * step * depth
            scratch[:tall, at : at + depth] = real
            scratch[:tall, at + depth : at + 2 * depth] = -imag
            scratch[tall:, at : at + depth] = imag
            scratch[tall:, at + depth : at + 2 * depth] = real
    dot = functools.partial(jnp.dot, preferred_element_type=jnp.float32)
    deep = slice(2 * depth * steps[0], 2 * depth * (steps[-1] + 1))
    for first in range(0, sites * cols, WIDE):
        at = (deep, slice(first, first + WIDE))
        total = dot(left_high[...], high_ref[at])
        total = total + dot(left_high[...], low_ref[at])
        total = total + dot(left_low[...], high_ref[at])
        for site in range(first // cols, (first + WIDE) // cols):
            across = slice(site * cols - first, site * cols - first + cols)
            for part in range(2):
                for op in range(ops):
                    start = part * tall + op * rows
                    value = total[start : start + rows, across]
                    if carried:
                        value = value + refs[count + 2][part, op, site]
                    out_ref[part, op, site] = value


def renorm(blocks, steps, high, low, carry, shape):
    blocks = [block if isinstance(block, tuple) else (block,) for block in blocks]
    blocks = blocks[steps.start : steps.stop]
    parts = tuple(len(block) for block in blocks)
    args = sum(blocks, ()) + (high, low) + (() if carry is None else (carry,))
    _, ops, sites, rows, cols = shape
    depth = blocks[0][0].shape[-1]
    left = pltpu.VMEM((2 * ops * rows, 2 * depth * len(blocks)), jnp.bfloat16)
    return pl.pallas_call(
        functools.partial(renorm_kernel, steps, parts, carry is not None),
        out_shape=tuple(jax.ShapeDtypeStruct(dims, jnp.float32) for dims in (shape, TILE)),
        in_specs=[VMEM] * len(args),
        out_specs=(VMEM, VMEM),
        scratch_shapes=[left, left],
        cost_estimate=pl.CostEstimate(
            flops=24 * ops * rows * depth * len(blocks) * sites * cols,
            bytes_accessed=4 << 20,
            transcendentals=0,
        ),
        compiler_params=pltpu.CompilerParams(vmem_limit_bytes=VMEM_BYTES),
    )(*args)


def total(parts, awaited):
    def kernel(*refs):
        refs[-1][...] = sum((ref[...] for ref in refs[1 : len(parts)]), refs[0][...])

    out = jax.ShapeDtypeStruct(parts[0].shape, parts[0].dtype)
    specs = [VMEM] * len(parts) + [ANY] * len(awaited)
    return call(kernel, out, specs, out.size * len(parts))(*parts, *awaited)


def combine_kernel(operators, tables, per, *refs):
    outs = refs[len(refs) - len(tables) :]
    comps, rows, _ = outs[0].shape[1:]
    me = lax.axis_index("pair")
    lane = lax.broadcasted_iota(jnp.int32, (1, TILE[1]), 1)
    for (held, under), out_ref in zip(tables, outs):
        for comp in range(comps):
            real = imag = None
            for array, place, op, key in operators:
                coefficients = []
                for part in range(2):
                    at = part * comps + comp
                    if under is None:
                        row = refs[held][at : at + 1, :]
                    else:
                        row = refs[held][under, 0, rows + at : rows + at + 1, :]
                    here = jnp.where(lane == (me ^ key) * per + op, row, 0.0)
                    coefficients.append(jnp.sum(here, axis=1, keepdims=True))
                cr, ci = coefficients
                br, bi = (refs[array][part, place, :rows, :] for part in range(2))
                tr, ti = cr * br - ci * bi, cr * bi + ci * br
                real = tr if real is None else real + tr
                imag = ti if imag is None else imag + ti
            out_ref[0, comp] = real
            out_ref[1, comp] = imag


def combine(arrays, operators, tables, per, shape, awaited=()):
    rows, cols = shape[2:]
    return call(
        functools.partial(combine_kernel, operators, tables, per),
        (jax.ShapeDtypeStruct(shape, jnp.float32),) * len(tables),
        [VMEM] * len(arrays) + [ANY] * len(awaited),
        8 * len(tables) * len(operators) * rows * cols,
    )(*arrays, *awaited)


def swap(x, axis, size, key):
    return lax.ppermute(x, axis, [(at, at ^ key) for at in range(size)])


def chip_blocks(own, row, pairs):
    per = own.shape[1]
    arrays, tables = [own], []
    operators = [(0, op, op, 0) for op in range(per)]
    if pairs == 8 and per == 2:
        for key in (2, 4):
            operators += [(len(arrays), op, op, key) for op in range(per)]
            arrays.append(swap(own, "pair", pairs, key))
        beside = swap(row, "pair", pairs, 2)
        operators += [(3, 0, 0, 6), (4, 0, 1, 6)]
        arrays += [
            swap(pack(arrays[1], range(1), [row, beside]), "pair", pairs, 4),
            swap(pack(arrays[2], range(1, 2), []), "pair", pairs, 2),
            row,
            beside,
        ]
        tables = [(5, None), (6, None), (3, 0), (3, 1)]
    else:
        arrays[0] = pack(own, range(per), [row])
        tables = [(0, 0)]
        for key in range(2, pairs, 2):
            operators += [(len(arrays), op, op, key) for op in range(per)]
            tables.append((len(arrays), 0))
            arrays.append(swap(arrays[0], "pair", pairs, key))
    return arrays, operators, tables


def on_device(pairs, sec, normal_ops, integrals, site_terms, basis):
    _, norms, rows, depth = normal_ops.shape
    _, sites, _, cols = basis.shape
    comps = integrals.shape[1]
    shape = (2, comps, rows, depth)
    two = swap(normal_ops, "sec", sec, 2)
    one = swap(normal_ops, "sec", sec, 1)
    row = tile(integrals)
    arrays, operators, tables = chip_blocks(normal_ops, row, pairs)
    high, low, site_part = prepare(basis, site_terms, rows, depth)
    two = after(after(two, high), one)
    three = swap(two, "sec", sec, 1)
    normals = [one, normal_ops, two, three]
    held = arrays + [row, swap(row, "pair", pairs, 1)]
    here = [(len(arrays), None), (len(arrays) + 1, None)]
    mine, other = combine(held, operators, here, norms, shape)
    comp_ops = total([mine, swap(other, "pair", pairs, 1)], [two])
    far = swap(comp_ops, "sec", sec, 3)
    near = swap(comp_ops, "sec", sec, 1)
    held = [two, swap(two, "pair", pairs, 1)] + arrays
    operators = [(key, op, op, key) for key in range(2) for op in range(norms)]
    tables = [(2 + at, part) for at, part in tables]
    parts = combine(held, operators, tables, norms, shape, [comp_ops])
    summed = [parts[0]] + [
        swap(part, "pair", pairs, key) for part, key in zip(parts[1:], range(2, pairs, 2))
    ]
    shape = (2, norms, sites, rows, cols)
    early, _ = renorm(normals, range(sec - 1), high, low, None, shape)
    new_normal, _ = renorm(normals, range(sec - 1, sec), high, low, early, shape)
    shape = (2, comps, sites, rows, cols)
    arrived = [near, comp_ops, tuple(summed), far]
    early, _ = renorm(arrived, range(1, sec), high, low, site_part, shape)
    return new_normal, renorm(arrived, range(1), high, low, early, shape)[0]


def solution(mesh):
    placed = (
        P(None, "pair", None, "sec"),
        P(None, "pair", None),
        P(None, "pair", None, None),
        P(None, None, None, "sec"),
    )
    return jax.shard_map(
        functools.partial(on_device, mesh.shape["pair"], mesh.shape["sec"]),
        mesh=mesh,
        in_specs=placed,
        out_specs=(P(None, "pair", None, None, "sec"), P(None, "pair", None, None, "sec")),
        check_vma=False,
    )
```

```python
import functools

import jax
import jax.numpy as jnp
from jax import lax
from jax.experimental import pallas as pl
from jax.experimental.pallas import tpu as pltpu
from jax.sharding import PartitionSpec as P

VMEM_BYTES = 24 * 1024 * 1024
WIDE = 256
TILE = (8, 128)
VMEM = pl.BlockSpec(memory_space=pltpu.VMEM)
ANY = pl.BlockSpec(memory_space=pl.ANY)
HBM = pl.BlockSpec(memory_space=pltpu.HBM)


def call(kernel, out_shape, in_specs, flops, scratch_shapes=()):
    return pl.pallas_call(
        kernel,
        out_shape=out_shape,
        in_specs=in_specs,
        out_specs=jax.tree.map(lambda _: VMEM, out_shape),
        scratch_shapes=scratch_shapes,
        cost_estimate=pl.CostEstimate(flops=flops, bytes_accessed=4 << 20, transcendentals=0),
        compiler_params=pltpu.CompilerParams(vmem_limit_bytes=VMEM_BYTES),
    )


def split(x):
    high = x.astype(jnp.bfloat16)
    return high, (x - high.astype(jnp.float32)).astype(jnp.bfloat16)


def order(sec):
    return (1, 0) + tuple(range(2, sec))


def prepare_kernel(depth, basis_hbm, site_hbm, _, high_ref, low_ref, part_ref, *scratch):
    basis_ref, site_ref, basis_sem, site_sem = scratch
    _, sites, old, cols = basis_ref.shape
    rows = part_ref.shape[3]
    me = lax.axis_index("sec")
    site_copy = pltpu.make_async_copy(site_hbm, site_ref, site_sem)
    site_copy.start()
    copies = [
        (part, site, pltpu.make_async_copy(
            basis_hbm.at[part, site], basis_ref.at[part, site], basis_sem.at[part, site]
        ))
        for part in range(2)
        for site in range(sites)
    ]
    for _, _, copy in copies:
        copy.start()
    for part, site, copy in copies:
        copy.wait()
        for step, far in enumerate(order(old // depth)):
            start = pl.multiple_of((me ^ far) * depth, depth)
            at = pl.ds((step * 2 + part) * depth, depth)
            high, low = split(basis_ref[part, site, pl.ds(start, depth), :])
            high_ref[at, pl.ds(site * cols, cols)] = high
            low_ref[at, pl.ds(site * cols, cols)] = low
    site_copy.wait()
    for comp in range(part_ref.shape[1]):
        for site in range(sites):
            real = imag = None
            for other in range(sites):
                sr, si = site_ref[0, comp, site, other], site_ref[1, comp, site, other]
                br, bi = basis_ref[0, other, :rows, :], basis_ref[1, other, :rows, :]
                tr, ti = sr * br - si * bi, sr * bi + si * br
                real = tr if real is None else real + tr
                imag = ti if imag is None else imag + ti
            part_ref[0, comp, site] = real
            part_ref[1, comp, site] = imag


def prepare(basis, site_terms, rows, depth, awaited):
    _, sites, old, cols = basis.shape
    comps = site_terms.shape[1]
    half = jax.ShapeDtypeStruct((2 * old, sites * cols), jnp.bfloat16)
    part = jax.ShapeDtypeStruct((2, comps, sites, rows, cols), jnp.float32)
    return call(
        functools.partial(prepare_kernel, depth),
        (half, half, part),
        [HBM, HBM, ANY],
        8 * comps * sites * sites * rows * cols,
        [
            pltpu.VMEM(basis.shape, basis.dtype),
            pltpu.SMEM(site_terms.shape, site_terms.dtype),
            pltpu.SemaphoreType.DMA((2, sites)),
            pltpu.SemaphoreType.DMA,
        ],
    )(basis, site_terms, awaited)


def tile(integrals):
    _, comps, norms = integrals.shape

    def kernel(integrals_ref, out_ref):
        out_ref[...] = jnp.zeros(TILE, jnp.float32)
        for part in range(2):
            out_ref[part * comps : (part + 1) * comps, :norms] = integrals_ref[part]

    return call(kernel, jax.ShapeDtypeStruct(TILE, jnp.float32), [VMEM], 0)(integrals)


def pack(block, ops, tiles):
    _, _, rows, cols = block.shape

    def kernel(block_ref, *refs):
        out_ref = refs[-1]
        out_ref[:, :, :rows, :] = block_ref[:, ops.start : ops.stop]
        out_ref[:, :, rows:, :] = jnp.zeros((2, len(ops)) + TILE, jnp.float32)
        for part, ref in enumerate(refs[:-1]):
            out_ref[part, 0, rows:, :] = ref[...]

    out = jax.ShapeDtypeStruct((2, len(ops), rows + TILE[0], cols), block.dtype)
    return call(kernel, out, [VMEM] * (1 + len(tiles)), 0)(block, *tiles)


def after(x, *others):
    def kernel(x_ref, *refs):
        refs[-1][...] = x_ref[...]

    out = jax.ShapeDtypeStruct(x.shape, x.dtype)
    return call(kernel, out, [VMEM] + [ANY] * len(others), 0)(x, *others)


def renorm_kernel(steps, parts, carried, streamed, *refs):
    count = sum(parts)
    high_ref, low_ref = refs[count : count + 2]
    out_ref, left_high, left_low = refs[count + 2 + carried : count + 5 + carried]
    out_hbm, out_ref, sems = (out_ref,) + refs[-2:] if streamed else (None, out_ref, None)
    _, ops, sites, rows, cols = out_ref.shape
    depth = refs[0].shape[-1]
    tall = ops * rows
    for step in range(len(steps)):
        first = sum(parts[:step])
        value = sum(refs[at][:, :, :rows, :] for at in range(first + 1, first + parts[step]))
        value = (refs[first][:, :, :rows, :] + value).reshape(2, tall, depth)
        for scratch, real, imag in zip((left_high, left_low), split(value[0]), split(value[1])):
            at = 2 * step * depth
            scratch[:tall, at : at + depth] = real
            scratch[:tall, at + depth : at + 2 * depth] = -imag
            scratch[tall:, at : at + depth] = imag
            scratch[tall:, at + depth : at + 2 * depth] = real
    dot = functools.partial(jnp.dot, preferred_element_type=jnp.float32)
    deep = slice(2 * depth * steps[0], 2 * depth * (steps[-1] + 1))
    copies = []
    for first in range(0, sites * cols, WIDE):
        at = (deep, slice(first, first + WIDE))
        total = dot(left_high[...], high_ref[at])
        total = total + dot(left_high[...], low_ref[at])
        total = total + dot(left_low[...], high_ref[at])
        some = range(first // cols, (first + WIDE) // cols)
        for part in range(2):
            for op in range(ops):
                for site in some:
                    across = slice(site * cols - first, site * cols - first + cols)
                    start = part * tall + op * rows
                    value = total[start : start + rows, across]
                    if carried:
                        value = value + refs[count + 2][part, op, site]
                    out_ref[part, op, site] = value
                if streamed:
                    piece = (part, op, pl.ds(some.start, len(some)))
                    copies.append(
                        pltpu.make_async_copy(
                            out_ref.at[piece], out_hbm.at[piece], sems.at[len(copies)]
                        )
                    )
                    copies[-1].start()
    for copy in copies:
        copy.wait()


def renorm(blocks, steps, high, low, carry, shape, streamed=False):
    blocks = [block if isinstance(block, tuple) else (block,) for block in blocks]
    blocks = blocks[steps.start : steps.stop]
    parts = tuple(len(block) for block in blocks)
    args = sum(blocks, ()) + (high, low) + (() if carry is None else (carry,))
    _, ops, sites, rows, cols = shape
    depth = blocks[0][0].shape[-1]
    left = pltpu.VMEM((2 * ops * rows, 2 * depth * len(blocks)), jnp.bfloat16)
    pieces = 2 * ops * sites * cols // WIDE
    held = [pltpu.VMEM(shape, jnp.float32), pltpu.SemaphoreType.DMA((pieces,))]
    return pl.pallas_call(
        functools.partial(renorm_kernel, steps, parts, carry is not None, streamed),
        out_shape=jax.ShapeDtypeStruct(shape, jnp.float32),
        in_specs=[VMEM] * len(args),
        out_specs=HBM if streamed else VMEM,
        scratch_shapes=[left, left] + (held if streamed else []),
        cost_estimate=pl.CostEstimate(
            flops=24 * ops * rows * depth * len(blocks) * sites * cols,
            bytes_accessed=4 << 20,
            transcendentals=0,
        ),
        compiler_params=pltpu.CompilerParams(vmem_limit_bytes=VMEM_BYTES),
    )(*args)


def total(parts, awaited):
    def kernel(*refs):
        refs[-1][...] = sum((ref[...] for ref in refs[1 : len(parts)]), refs[0][...])

    out = jax.ShapeDtypeStruct(parts[0].shape, parts[0].dtype)
    specs = [VMEM] * len(parts) + [ANY] * len(awaited)
    return call(kernel, out, specs, out.size * len(parts))(*parts, *awaited)


def combine_kernel(operators, tables, per, *refs):
    outs = refs[len(refs) - len(tables) :]
    comps, rows, _ = outs[0].shape[1:]
    me = lax.axis_index("pair")
    lane = lax.broadcasted_iota(jnp.int32, (1, TILE[1]), 1)
    for (held, under), out_ref in zip(tables, outs):
        for comp in range(comps):
            real = imag = None
            for array, place, op, key in operators:
                coefficients = []
                for part in range(2):
                    at = part * comps + comp
                    if under is None:
                        row = refs[held][at : at + 1, :]
                    else:
                        row = refs[held][under, 0, rows + at : rows + at + 1, :]
                    here = jnp.where(lane == (me ^ key) * per + op, row, 0.0)
                    coefficients.append(jnp.sum(here, axis=1, keepdims=True))
                cr, ci = coefficients
                br, bi = (refs[array][part, place, :rows, :] for part in range(2))
                tr, ti = cr * br - ci * bi, cr * bi + ci * br
                real = tr if real is None else real + tr
                imag = ti if imag is None else imag + ti
            out_ref[0, comp] = real
            out_ref[1, comp] = imag


def combine(arrays, operators, tables, per, shape, awaited=()):
    rows, cols = shape[2:]
    return call(
        functools.partial(combine_kernel, operators, tables, per),
        (jax.ShapeDtypeStruct(shape, jnp.float32),) * len(tables),
        [VMEM] * len(arrays) + [ANY] * len(awaited),
        8 * len(tables) * len(operators) * rows * cols,
    )(*arrays, *awaited)


def swap(x, axis, size, key):
    return lax.ppermute(x, axis, [(at, at ^ key) for at in range(size)])


def chip_blocks(own, row, pairs):
    per = own.shape[1]
    arrays, tables = [own], []
    operators = [(0, op, op, 0) for op in range(per)]
    if pairs == 8:
        for key in (2, 4):
            operators += [(len(arrays), op, op, key) for op in range(per)]
            arrays.append(swap(own, "pair", pairs, key))
        beside = swap(row, "pair", pairs, 2)
        operators += [(3, op, op, 6) for op in range(per)]
        arrays += [
            swap(pack(arrays[1], range(per), [row, beside]), "pair", pairs, 4),
            row,
            beside,
        ]
        tables = [(4, None), (5, None), (3, 0), (3, 1)]
    else:
        arrays[0] = pack(own, range(per), [row])
        tables = [(0, 0)]
        for key in range(2, pairs, 2):
            operators += [(len(arrays), op, op, key) for op in range(per)]
            tables.append((len(arrays), 0))
            arrays.append(swap(arrays[0], "pair", pairs, key))
    return arrays, operators, tables


def on_device(pairs, sec, normal_ops, integrals, site_terms, basis):
    _, norms, rows, depth = normal_ops.shape
    _, sites, _, cols = basis.shape
    comps = integrals.shape[1]
    shape = (2, comps, rows, depth)
    two = swap(normal_ops, "sec", sec, 2)
    one = swap(normal_ops, "sec", sec, 1)
    row = tile(integrals)
    arrays, operators, tables = chip_blocks(normal_ops, row, pairs)
    sibling = swap(row, "pair", pairs, 1)
    high, low, site_part = prepare(basis, site_terms, rows, depth, sibling)
    two = after(after(after(two, high), arrays[2]), one)
    three = swap(two, "sec", sec, 1)
    normals = [one, normal_ops, two, three]
    held = arrays + [row, sibling]
    here = [(len(arrays), None), (len(arrays) + 1, None)]
    mine, other = combine(held, operators, here, norms, shape)
    held = [two, swap(two, "pair", pairs, 1)] + arrays
    operators = [(key, op, op, key) for key in range(2) for op in range(norms)]
    tables = [(2 + at, part) for at, part in tables]
    parts = combine(held, operators, tables, norms, shape)
    comp_ops = total([mine, swap(other, "pair", pairs, 1)], [parts[0]])
    far = swap(comp_ops, "sec", sec, 3)
    near = swap(after(comp_ops, three), "sec", sec, 1)
    summed = [parts[0]] + [
        swap(part, "pair", pairs, key) for part, key in zip(parts[1:], range(2, pairs, 2))
    ]
    shape = (2, norms, sites, rows, cols)
    early = renorm(normals, range(sec - 1), high, low, None, shape)
    new_normal = renorm(normals, range(sec - 1, sec), high, low, early, shape, True)
    shape = (2, comps, sites, rows, cols)
    arrived = [near, comp_ops, tuple(summed), far]
    early = renorm(arrived, range(1, sec), high, low, site_part, shape)
    return new_normal, renorm(arrived, range(1), high, low, early, shape, True)


def solution(mesh):
    placed = (
        P(None, "pair", None, "sec"),
        P(None, "pair", None),
        P(None, "pair", None, None),
        P(None, None, None, "sec"),
    )
    return jax.shard_map(
        functools.partial(on_device, mesh.shape["pair"], mesh.shape["sec"]),
        mesh=mesh,
        in_specs=placed,
        out_specs=(P(None, "pair", None, None, "sec"), P(None, "pair", None, None, "sec")),
        check_vma=False,
    )
```

```python
import functools

import jax
import jax.numpy as jnp
from jax import lax
from jax.experimental import pallas as pl
from jax.experimental.pallas import tpu as pltpu
from jax.sharding import PartitionSpec as P

VMEM_BYTES = 24 * 1024 * 1024
WIDE = 256
TILE = (8, 128)
VMEM = pl.BlockSpec(memory_space=pltpu.VMEM)
ANY = pl.BlockSpec(memory_space=pl.ANY)
HBM = pl.BlockSpec(memory_space=pltpu.HBM)


def call(kernel, out_shape, in_specs, flops, scratch_shapes=()):
    return pl.pallas_call(
        kernel,
        out_shape=out_shape,
        in_specs=in_specs,
        out_specs=jax.tree.map(lambda _: VMEM, out_shape),
        scratch_shapes=scratch_shapes,
        cost_estimate=pl.CostEstimate(flops=flops, bytes_accessed=4 << 20, transcendentals=0),
        compiler_params=pltpu.CompilerParams(vmem_limit_bytes=VMEM_BYTES),
    )


def split(x):
    high = x.astype(jnp.bfloat16)
    return high, (x - high.astype(jnp.float32)).astype(jnp.bfloat16)


def order(sec):
    return (1, 2, 0) + tuple(range(3, sec))


def prepare_kernel(depth, basis_hbm, site_hbm, _, high_ref, low_ref, part_ref, *scratch):
    basis_ref, site_ref, basis_sem, site_sem = scratch
    _, sites, old, cols = basis_ref.shape
    rows = part_ref.shape[3]
    me = lax.axis_index("sec")
    site_copy = pltpu.make_async_copy(site_hbm, site_ref, site_sem)
    site_copy.start()
    copies = [
        (part, site, pltpu.make_async_copy(
            basis_hbm.at[part, site], basis_ref.at[part, site], basis_sem.at[part, site]
        ))
        for part in range(2)
        for site in range(sites)
    ]
    for _, _, copy in copies:
        copy.start()
    for part, site, copy in copies:
        copy.wait()
        for step, far in enumerate(order(old // depth)):
            start = pl.multiple_of((me ^ far) * depth, depth)
            at = pl.ds((step * 2 + part) * depth, depth)
            high, low = split(basis_ref[part, site, pl.ds(start, depth), :])
            high_ref[at, pl.ds(site * cols, cols)] = high
            low_ref[at, pl.ds(site * cols, cols)] = low
    site_copy.wait()
    for comp in range(part_ref.shape[1]):
        for site in range(sites):
            real = imag = None
            for other in range(sites):
                sr, si = site_ref[0, comp, site, other], site_ref[1, comp, site, other]
                br, bi = basis_ref[0, other, :rows, :], basis_ref[1, other, :rows, :]
                tr, ti = sr * br - si * bi, sr * bi + si * br
                real = tr if real is None else real + tr
                imag = ti if imag is None else imag + ti
            part_ref[0, comp, site] = real
            part_ref[1, comp, site] = imag


def prepare(basis, site_terms, rows, depth, awaited):
    _, sites, old, cols = basis.shape
    comps = site_terms.shape[1]
    half = jax.ShapeDtypeStruct((2 * old, sites * cols), jnp.bfloat16)
    part = jax.ShapeDtypeStruct((2, comps, sites, rows, cols), jnp.float32)
    return call(
        functools.partial(prepare_kernel, depth),
        (half, half, part),
        [HBM, HBM, ANY],
        8 * comps * sites * sites * rows * cols,
        [
            pltpu.VMEM(basis.shape, basis.dtype),
            pltpu.SMEM(site_terms.shape, site_terms.dtype),
            pltpu.SemaphoreType.DMA((2, sites)),
            pltpu.SemaphoreType.DMA,
        ],
    )(basis, site_terms, awaited)


def pack(block, tables):
    _, per, rows, cols = block.shape

    def kernel(block_ref, *refs):
        out_ref = refs[-1]
        out_ref[:, :, :rows, :] = block_ref[...]
        out_ref[:, :, rows:, :] = jnp.zeros((2, per) + TILE, jnp.float32)
        for under, ref in enumerate(refs[:-1]):
            _, comps, norms = ref.shape
            for part in range(2):
                first = rows + part * comps
                out_ref[under, 0, first : first + comps, :norms] = ref[part]

    out = jax.ShapeDtypeStruct((2, per, rows + TILE[0], cols), block.dtype)
    return call(kernel, out, [VMEM] * (1 + len(tables)), 0)(block, *tables)


def after(x, *others):
    def kernel(x_ref, *refs):
        refs[-1][...] = x_ref[...]

    out = jax.ShapeDtypeStruct(x.shape, x.dtype)
    return call(kernel, out, [VMEM] + [ANY] * len(others), 0)(x, *others)


def renorm_kernel(steps, parts, carried, streamed, *refs):
    count = sum(parts)
    high_ref, low_ref = refs[count : count + 2]
    out_ref, left_high, left_low = refs[count + 2 + carried : count + 5 + carried]
    out_hbm, out_ref, sems = (out_ref,) + refs[-2:] if streamed else (None, out_ref, None)
    _, ops, sites, rows, cols = out_ref.shape
    depth = refs[0].shape[-1]
    tall = ops * rows
    for step in range(len(steps)):
        first = sum(parts[:step])
        value = sum(refs[at][:, :, :rows, :] for at in range(first + 1, first + parts[step]))
        value = (refs[first][:, :, :rows, :] + value).reshape(2, tall, depth)
        for scratch, real, imag in zip((left_high, left_low), split(value[0]), split(value[1])):
            at = 2 * step * depth
            scratch[:tall, at : at + depth] = real
            scratch[:tall, at + depth : at + 2 * depth] = -imag
            scratch[tall:, at : at + depth] = imag
            scratch[tall:, at + depth : at + 2 * depth] = real
    dot = functools.partial(jnp.dot, preferred_element_type=jnp.float32)
    deep = slice(2 * depth * steps[0], 2 * depth * (steps[-1] + 1))
    copies = []
    for first in range(0, sites * cols, WIDE):
        at = (deep, slice(first, first + WIDE))
        total = dot(left_high[...], high_ref[at])
        total = total + dot(left_high[...], low_ref[at])
        total = total + dot(left_low[...], high_ref[at])
        some = range(first // cols, (first + WIDE) // cols)
        for part in range(2):
            for op in range(ops):
                for site in some:
                    across = slice(site * cols - first, site * cols - first + cols)
                    start = part * tall + op * rows
                    value = total[start : start + rows, across]
                    if carried:
                        value = value + refs[count + 2][part, op, site]
                    out_ref[part, op, site] = value
                if streamed:
                    piece = (part, op, pl.ds(some.start, len(some)))
                    copies.append(
                        pltpu.make_async_copy(
                            out_ref.at[piece], out_hbm.at[piece], sems.at[len(copies)]
                        )
                    )
                    copies[-1].start()
    for copy in copies:
        copy.wait()


def renorm(blocks, steps, high, low, carry, shape, streamed=False):
    blocks = [block if isinstance(block, tuple) else (block,) for block in blocks]
    blocks = blocks[steps.start : steps.stop]
    parts = tuple(len(block) for block in blocks)
    args = sum(blocks, ()) + (high, low) + (() if carry is None else (carry,))
    _, ops, sites, rows, cols = shape
    depth = blocks[0][0].shape[-1]
    left = pltpu.VMEM((2 * ops * rows, 2 * depth * len(blocks)), jnp.bfloat16)
    pieces = 2 * ops * sites * cols // WIDE
    held = [pltpu.VMEM(shape, jnp.float32), pltpu.SemaphoreType.DMA((pieces,))]
    return pl.pallas_call(
        functools.partial(renorm_kernel, steps, parts, carry is not None, streamed),
        out_shape=jax.ShapeDtypeStruct(shape, jnp.float32),
        in_specs=[VMEM] * len(args),
        out_specs=HBM if streamed else VMEM,
        scratch_shapes=[left, left] + (held if streamed else []),
        cost_estimate=pl.CostEstimate(
            flops=24 * ops * rows * depth * len(blocks) * sites * cols,
            bytes_accessed=4 << 20,
            transcendentals=0,
        ),
        compiler_params=pltpu.CompilerParams(vmem_limit_bytes=VMEM_BYTES),
    )(*args)


def total(parts, awaited):
    def kernel(*refs):
        refs[-1][...] = sum((ref[...] for ref in refs[1 : len(parts)]), refs[0][...])

    out = jax.ShapeDtypeStruct(parts[0].shape, parts[0].dtype)
    specs = [VMEM] * len(parts) + [ANY] * len(awaited)
    return call(kernel, out, specs, out.size * len(parts))(*parts, *awaited)


def combine_kernel(operators, tables, per, *refs):
    outs = refs[len(refs) - len(tables) :]
    comps, rows, _ = outs[0].shape[1:]
    me = lax.axis_index("pair")
    for (held, under), out_ref in zip(tables, outs):
        lane = lax.broadcasted_iota(jnp.int32, (1, refs[held].shape[-1]), 1)
        for comp in range(comps):
            real = imag = None
            for array, place, op, key in operators:
                coefficients = []
                for part in range(2):
                    at = part * comps + comp
                    if under is None:
                        row = refs[held][part, comp : comp + 1, :]
                    else:
                        row = refs[held][under, 0, rows + at : rows + at + 1, :]
                    here = jnp.where(lane == (me ^ key) * per + op, row, 0.0)
                    coefficients.append(jnp.sum(here, axis=1, keepdims=True))
                cr, ci = coefficients
                br, bi = (refs[array][part, place, :rows, :] for part in range(2))
                tr, ti = cr * br - ci * bi, cr * bi + ci * br
                real = tr if real is None else real + tr
                imag = ti if imag is None else imag + ti
            out_ref[0, comp] = real
            out_ref[1, comp] = imag


def combine(arrays, operators, tables, per, shape, awaited=()):
    rows, cols = shape[2:]
    return call(
        functools.partial(combine_kernel, operators, tables, per),
        (jax.ShapeDtypeStruct(shape, jnp.float32),) * len(tables),
        [VMEM] * len(arrays) + [ANY] * len(awaited),
        8 * len(tables) * len(operators) * rows * cols,
    )(*arrays, *awaited)


def swap(x, axis, size, key):
    return lax.ppermute(x, axis, [(at, at ^ key) for at in range(size)])


def chip_blocks(own, row, pairs):
    per = own.shape[1]
    arrays, tables = [own], []
    operators = [(0, op, op, 0) for op in range(per)]
    if pairs == 8:
        for key in (2, 4):
            operators += [(len(arrays), op, op, key) for op in range(per)]
            arrays.append(swap(own, "pair", pairs, key))
        beside = swap(row, "pair", pairs, 2)
        operators += [(3, op, op, 6) for op in range(per)]
        arrays += [
            swap(pack(arrays[1], [row, beside]), "pair", pairs, 4),
            row,
            beside,
        ]
        tables = [(4, None), (5, None), (3, 0), (3, 1)]
    else:
        arrays[0] = pack(own, [row])
        tables = [(0, 0)]
        for key in range(2, pairs, 2):
            operators += [(len(arrays), op, op, key) for op in range(per)]
            tables.append((len(arrays), 0))
            arrays.append(swap(arrays[0], "pair", pairs, key))
    return arrays, operators, tables


def on_device(pairs, sec, normal_ops, integrals, site_terms, basis):
    _, norms, rows, depth = normal_ops.shape
    _, sites, _, cols = basis.shape
    comps = integrals.shape[1]
    shape = (2, comps, rows, depth)
    two = swap(normal_ops, "sec", sec, 2)
    one = swap(normal_ops, "sec", sec, 1)
    arrays, operators, tables = chip_blocks(normal_ops, integrals, pairs)
    sibling = swap(integrals, "pair", pairs, 1)
    high, low, site_part = prepare(basis, site_terms, rows, depth, sibling)
    two = after(two, high)
    three = swap(two, "sec", sec, 1)
    two = after(after(two, arrays[2]), one)
    normals = [one, two, normal_ops, three]
    held = arrays + [integrals, sibling]
    here = [(len(arrays), None), (len(arrays) + 1, None)]
    mine, other = combine(held, operators, here, norms, shape)
    held = [two, swap(two, "pair", pairs, 1)] + arrays
    operators = [(key, op, op, key) for key in range(2) for op in range(norms)]
    tables = [(2 + at, part) for at, part in tables]
    parts = combine(held, operators, tables, norms, shape)
    comp_ops = total([mine, swap(other, "pair", pairs, 1)], [parts[0]])
    far = swap(comp_ops, "sec", sec, 3)
    near = swap(after(comp_ops, three), "sec", sec, 1)
    summed = [parts[0]] + [
        swap(after(part, comp_ops), "pair", pairs, key)
        for part, key in zip(parts[1:], range(2, pairs, 2))
    ]
    shape = (2, norms, sites, rows, cols)
    early = renorm(normals, range(sec - 1), high, low, None, shape)
    new_normal = renorm(normals, range(sec - 1, sec), high, low, early, shape, True)
    shape = (2, comps, sites, rows, cols)
    arrived = [near, tuple(summed), comp_ops, far]
    early = renorm(arrived, range(2, sec), high, low, site_part, shape)
    early = renorm(arrived, range(1, 2), high, low, early, shape)
    return new_normal, renorm(arrived, range(1), high, low, early, shape, True)


def solution(mesh):
    placed = (
        P(None, "pair", None, "sec"),
        P(None, "pair", None),
        P(None, "pair", None, None),
        P(None, None, None, "sec"),
    )
    return jax.shard_map(
        functools.partial(on_device, mesh.shape["pair"], mesh.shape["sec"]),
        mesh=mesh,
        in_specs=placed,
        out_specs=(P(None, "pair", None, None, "sec"), P(None, "pair", None, None, "sec")),
        check_vma=False,
    )
```

```python
import functools

import jax
import jax.numpy as jnp
from jax import lax
from jax.experimental import pallas as pl
from jax.experimental.pallas import tpu as pltpu
from jax.sharding import PartitionSpec as P

VMEM_BYTES = 24 * 1024 * 1024
WIDE = 256
TILE = (8, 128)
VMEM = pl.BlockSpec(memory_space=pltpu.VMEM)
ANY = pl.BlockSpec(memory_space=pl.ANY)
HBM = pl.BlockSpec(memory_space=pltpu.HBM)


def call(kernel, out_shape, in_specs, flops, scratch_shapes=()):
    return pl.pallas_call(
        kernel,
        out_shape=out_shape,
        in_specs=in_specs,
        out_specs=jax.tree.map(lambda _: VMEM, out_shape),
        scratch_shapes=scratch_shapes,
        cost_estimate=pl.CostEstimate(flops=flops, bytes_accessed=4 << 20, transcendentals=0),
        compiler_params=pltpu.CompilerParams(vmem_limit_bytes=VMEM_BYTES),
    )


def split(x):
    high = x.astype(jnp.bfloat16)
    return high, (x - high.astype(jnp.float32)).astype(jnp.bfloat16)


def order(sec):
    return (3, 1, 0, 2) if sec == 4 else tuple(range(sec))


def prepare_kernel(depth, basis_hbm, site_hbm, integrals_ref, *refs):
    high_ref, low_ref, part_ref, row_ref = refs[:4]
    scratch = refs[4:]
    row_ref[...] = integrals_ref[...]
    basis_ref, site_ref, basis_sem, site_sem = scratch
    _, sites, old, cols = basis_ref.shape
    rows = part_ref.shape[3]
    me = lax.axis_index("sec")
    site_copy = pltpu.make_async_copy(site_hbm, site_ref, site_sem)
    site_copy.start()
    copies = [
        (part, site, pltpu.make_async_copy(
            basis_hbm.at[part, site], basis_ref.at[part, site], basis_sem.at[part, site]
        ))
        for part in range(2)
        for site in range(sites)
    ]
    for _, _, copy in copies:
        copy.start()
    for part, site, copy in copies:
        copy.wait()
        for step, far in enumerate(order(old // depth)):
            start = pl.multiple_of((me ^ far) * depth, depth)
            at = pl.ds((step * 2 + part) * depth, depth)
            high, low = split(basis_ref[part, site, pl.ds(start, depth), :])
            high_ref[at, pl.ds(site * cols, cols)] = high
            low_ref[at, pl.ds(site * cols, cols)] = low
    site_copy.wait()
    for comp in range(part_ref.shape[1]):
        for site in range(sites):
            real = imag = None
            for other in range(sites):
                sr, si = site_ref[0, comp, site, other], site_ref[1, comp, site, other]
                br, bi = basis_ref[0, other, :rows, :], basis_ref[1, other, :rows, :]
                tr, ti = sr * br - si * bi, sr * bi + si * br
                real = tr if real is None else real + tr
                imag = ti if imag is None else imag + ti
            part_ref[0, comp, site] = real
            part_ref[1, comp, site] = imag


def prepare(basis, site_terms, integrals, rows, depth):
    _, sites, old, cols = basis.shape
    comps = site_terms.shape[1]
    half = jax.ShapeDtypeStruct((2 * old, sites * cols), jnp.bfloat16)
    part = jax.ShapeDtypeStruct((2, comps, sites, rows, cols), jnp.float32)
    return call(
        functools.partial(prepare_kernel, depth),
        (half, half, part, jax.ShapeDtypeStruct(integrals.shape, integrals.dtype)),
        [HBM, HBM, VMEM],
        8 * comps * sites * sites * rows * cols,
        [
            pltpu.VMEM(basis.shape, basis.dtype),
            pltpu.SMEM(site_terms.shape, site_terms.dtype),
            pltpu.SemaphoreType.DMA((2, sites)),
            pltpu.SemaphoreType.DMA,
        ],
    )(basis, site_terms, integrals)


def pack(block, tables):
    _, per, rows, cols = block.shape

    def kernel(block_ref, *refs):
        out_ref = refs[-1]
        out_ref[:, :, :rows, :] = block_ref[...]
        out_ref[:, :, rows:, :] = jnp.zeros((2, per) + TILE, jnp.float32)
        for under, ref in enumerate(refs[:-1]):
            _, comps, norms = ref.shape
            for part in range(2):
                first = rows + part * comps
                out_ref[under, 0, first : first + comps, :norms] = ref[part]

    out = jax.ShapeDtypeStruct((2, per, rows + TILE[0], cols), block.dtype)
    return call(kernel, out, [VMEM] * (1 + len(tables)), 0)(block, *tables)


def after(x, *others):
    def kernel(x_ref, *refs):
        refs[-1][...] = x_ref[...]

    out = jax.ShapeDtypeStruct(x.shape, x.dtype)
    return call(kernel, out, [VMEM] + [ANY] * len(others), 0)(x, *others)


def renorm_kernel(steps, parts, carried, streamed, *refs):
    count = sum(parts)
    high_ref, low_ref = refs[count : count + 2]
    out_ref, left_high, left_low = refs[count + 2 + carried : count + 5 + carried]
    out_hbm, out_ref, sems = (out_ref,) + refs[-2:] if streamed else (None, out_ref, None)
    _, ops, sites, rows, cols = out_ref.shape
    depth = refs[0].shape[-1]
    tall = ops * rows
    for step in range(len(steps)):
        first = sum(parts[:step])
        value = sum(refs[at][:, :, :rows, :] for at in range(first + 1, first + parts[step]))
        value = (refs[first][:, :, :rows, :] + value).reshape(2, tall, depth)
        for scratch, real, imag in zip((left_high, left_low), split(value[0]), split(value[1])):
            at = 2 * step * depth
            scratch[:tall, at : at + depth] = real
            scratch[:tall, at + depth : at + 2 * depth] = -imag
            scratch[tall:, at : at + depth] = imag
            scratch[tall:, at + depth : at + 2 * depth] = real
    dot = functools.partial(jnp.dot, preferred_element_type=jnp.float32)
    deep = slice(2 * depth * steps[0], 2 * depth * (steps[-1] + 1))
    copies = []
    for first in range(0, sites * cols, WIDE):
        at = (deep, slice(first, first + WIDE))
        total = dot(left_high[...], high_ref[at])
        total = total + dot(left_high[...], low_ref[at])
        total = total + dot(left_low[...], high_ref[at])
        some = range(first // cols, (first + WIDE) // cols)
        for part in range(2):
            for op in range(ops):
                for site in some:
                    across = slice(site * cols - first, site * cols - first + cols)
                    start = part * tall + op * rows
                    value = total[start : start + rows, across]
                    if carried:
                        value = value + refs[count + 2][part, op, site]
                    out_ref[part, op, site] = value
                if streamed:
                    piece = (part, op, pl.ds(some.start, len(some)))
                    copies.append(
                        pltpu.make_async_copy(
                            out_ref.at[piece], out_hbm.at[piece], sems.at[len(copies)]
                        )
                    )
                    copies[-1].start()
    for copy in copies:
        copy.wait()


def renorm(blocks, steps, high, low, carry, shape, streamed=False):
    blocks = [block if isinstance(block, tuple) else (block,) for block in blocks]
    blocks = blocks[steps.start : steps.stop]
    parts = tuple(len(block) for block in blocks)
    args = sum(blocks, ()) + (high, low) + (() if carry is None else (carry,))
    _, ops, sites, rows, cols = shape
    depth = blocks[0][0].shape[-1]
    left = pltpu.VMEM((2 * ops * rows, 2 * depth * len(blocks)), jnp.bfloat16)
    pieces = 2 * ops * sites * cols // WIDE
    held = [pltpu.VMEM(shape, jnp.float32), pltpu.SemaphoreType.DMA((pieces,))]
    return pl.pallas_call(
        functools.partial(renorm_kernel, steps, parts, carry is not None, streamed),
        out_shape=jax.ShapeDtypeStruct(shape, jnp.float32),
        in_specs=[VMEM] * len(args),
        out_specs=HBM if streamed else VMEM,
        scratch_shapes=[left, left] + (held if streamed else []),
        cost_estimate=pl.CostEstimate(
            flops=24 * ops * rows * depth * len(blocks) * sites * cols,
            bytes_accessed=4 << 20,
            transcendentals=0,
        ),
        compiler_params=pltpu.CompilerParams(vmem_limit_bytes=VMEM_BYTES),
    )(*args)


def first_rows(block, count):
    _, norms, rows, cols = block.shape

    def kernel(block_ref, out_ref):
        for at in range(count):
            out_ref[at] = block_ref[at // norms, at % norms]

    return call(kernel, jax.ShapeDtypeStruct((count, rows, cols), block.dtype), [VMEM], 0)(block)


def total(mine, other, block, count, awaited):
    _, norms, rows, cols = block.shape
    comps = mine.shape[1]
    left = 2 * norms - count

    def kernel(mine_ref, other_ref, block_ref, _, sum_ref, both_ref):
        for at in range(left):
            both_ref[at] = block_ref[(count + at) // norms, (count + at) % norms]
        for part in range(2):
            value = mine_ref[part] + other_ref[part]
            sum_ref[part] = value
            both_ref[left + part * comps : left + (part + 1) * comps] = value

    out = (
        jax.ShapeDtypeStruct(mine.shape, mine.dtype),
        jax.ShapeDtypeStruct((left + 2 * comps, rows, cols), mine.dtype),
    )
    return call(kernel, out, [VMEM] * 3 + [ANY], mine.size)(mine, other, block, awaited)


def unpack(first, both, norms):
    count, rows, cols = first.shape
    left = 2 * norms - count
    comps = (both.shape[0] - left) // 2

    def kernel(first_ref, both_ref, block_ref, sum_ref):
        for at in range(2 * norms):
            value = first_ref[at] if at < count else both_ref[at - count]
            block_ref[at // norms, at % norms] = value
        for part in range(2):
            sum_ref[part] = both_ref[left + part * comps : left + (part + 1) * comps]

    out = tuple(jax.ShapeDtypeStruct((2, n, rows, cols), first.dtype) for n in (norms, comps))
    return call(kernel, out, [VMEM] * 2, 0)(first, both)


def combine_kernel(operators, tables, per, *refs):
    outs = refs[len(refs) - len(tables) :]
    comps, rows, _ = outs[0].shape[1:]
    me = lax.axis_index("pair")
    for (held, under), out_ref in zip(tables, outs):
        lane = lax.broadcasted_iota(jnp.int32, (1, refs[held].shape[-1]), 1)
        for comp in range(comps):
            real = imag = None
            for array, place, op, key in operators:
                coefficients = []
                for part in range(2):
                    at = part * comps + comp
                    if under is None:
                        row = refs[held][part, comp : comp + 1, :]
                    else:
                        row = refs[held][under, 0, rows + at : rows + at + 1, :]
                    here = jnp.where(lane == (me ^ key) * per + op, row, 0.0)
                    coefficients.append(jnp.sum(here, axis=1, keepdims=True))
                cr, ci = coefficients
                br, bi = (refs[array][part, place, :rows, :] for part in range(2))
                tr, ti = cr * br - ci * bi, cr * bi + ci * br
                real = tr if real is None else real + tr
                imag = ti if imag is None else imag + ti
            out_ref[0, comp] = real
            out_ref[1, comp] = imag


def combine(arrays, operators, tables, per, shape, awaited=()):
    rows, cols = shape[2:]
    return call(
        functools.partial(combine_kernel, operators, tables, per),
        (jax.ShapeDtypeStruct(shape, jnp.float32),) * len(tables),
        [VMEM] * len(arrays) + [ANY] * len(awaited),
        8 * len(tables) * len(operators) * rows * cols,
    )(*arrays, *awaited)


def swap(x, axis, size, key):
    return lax.ppermute(x, axis, [(at, at ^ key) for at in range(size)])


def chip_blocks(own, row, beside, pairs):
    per = own.shape[1]
    arrays, tables = [own], []
    operators = [(0, op, op, 0) for op in range(per)]
    if pairs == 8:
        for key in (2, 4):
            operators += [(len(arrays), op, op, key) for op in range(per)]
            arrays.append(swap(own, "pair", pairs, key))
        operators += [(3, op, op, 6) for op in range(per)]
        arrays += [
            swap(pack(arrays[1], [row, beside]), "pair", pairs, 4),
            row,
            beside,
        ]
        tables = [(4, None), (5, None), (3, 0), (3, 1)]
    else:
        arrays[0] = pack(own, [row])
        tables = [(0, 0)]
        for key in range(2, pairs, 2):
            operators += [(len(arrays), op, op, key) for op in range(per)]
            tables.append((len(arrays), 0))
            arrays.append(swap(arrays[0], "pair", pairs, key))
    return arrays, operators, tables


def on_device(pairs, sec, normal_ops, integrals, site_terms, basis):
    _, norms, rows, depth = normal_ops.shape
    _, sites, _, cols = basis.shape
    comps = integrals.shape[1]
    shape = (2, comps, rows, depth)
    two = swap(normal_ops, "sec", sec, 2)
    one = swap(normal_ops, "sec", sec, 1)
    beside = swap(integrals, "pair", pairs, 2)
    sibling = swap(integrals, "pair", pairs, 1)
    high, low, site_part, row = prepare(basis, site_terms, integrals, rows, depth)
    arrays, operators, tables = chip_blocks(normal_ops, row, beside, pairs)
    two = after(two, sibling)
    count = 2 * norms - 1
    three_first = swap(first_rows(two, count), "sec", sec, 1)
    two = after(after(two, arrays[2]), one)
    held = arrays + [row, sibling]
    here = [(len(arrays), None), (len(arrays) + 1, None)]
    mine, other = combine(held, operators, here, norms, shape)
    held = [two, swap(two, "pair", pairs, 1)] + arrays
    operators = [(key, op, op, key) for key in range(2) for op in range(norms)]
    tables = [(2 + at, part) for at, part in tables]
    parts = combine(held, operators, tables, norms, shape)
    comp_ops, both = total(mine, swap(other, "pair", pairs, 1), two, count, parts[0])
    both = swap(both, "sec", sec, 1)
    at_two = [parts[0]]
    for key in range(2, pairs, 2):
        part = after(parts[key // 2], comp_ops)
        if key < pairs - 2:
            part = after(part, three_first)
        at_two.append(swap(part, "pair", pairs, key))
    far = swap(comp_ops, "sec", sec, 3)
    three, near = unpack(three_first, both, norms)
    normals = [three, one, normal_ops, two]
    shape = (2, norms, sites, rows, cols)
    early = renorm(normals, range(1, sec), high, low, None, shape)
    new_normal = renorm(normals, range(1), high, low, early, shape, True)
    shape = (2, comps, sites, rows, cols)
    arrived = [far, near, comp_ops, tuple(at_two)]
    early = renorm(arrived, range(2, sec), high, low, site_part, shape)
    early = renorm(arrived, range(1, 2), high, low, early, shape)
    return new_normal, renorm(arrived, range(1), high, low, early, shape, True)


def solution(mesh):
    placed = (
        P(None, "pair", None, "sec"),
        P(None, "pair", None),
        P(None, "pair", None, None),
        P(None, None, None, "sec"),
    )
    return jax.shard_map(
        functools.partial(on_device, mesh.shape["pair"], mesh.shape["sec"]),
        mesh=mesh,
        in_specs=placed,
        out_specs=(P(None, "pair", None, None, "sec"), P(None, "pair", None, None, "sec")),
        check_vma=False,
    )
```

```python
import functools

import jax
import jax.numpy as jnp
from jax import lax
from jax.experimental import pallas as pl
from jax.experimental.pallas import tpu as pltpu
from jax.sharding import PartitionSpec as P

VMEM_BYTES = 24 * 1024 * 1024
WIDE = 256
TILE = (8, 128)
VMEM = pl.BlockSpec(memory_space=pltpu.VMEM)
ANY = pl.BlockSpec(memory_space=pl.ANY)
HBM = pl.BlockSpec(memory_space=pltpu.HBM)


def call(kernel, out_shape, in_specs, flops, scratch_shapes=()):
    return pl.pallas_call(
        kernel,
        out_shape=out_shape,
        in_specs=in_specs,
        out_specs=jax.tree.map(lambda _: VMEM, out_shape),
        scratch_shapes=scratch_shapes,
        cost_estimate=pl.CostEstimate(flops=flops, bytes_accessed=4 << 20, transcendentals=0),
        compiler_params=pltpu.CompilerParams(vmem_limit_bytes=VMEM_BYTES),
    )


def split(x):
    high = x.astype(jnp.bfloat16)
    return high, (x - high.astype(jnp.float32)).astype(jnp.bfloat16)


def order(sec):
    return (3, 1, 0, 2) if sec == 4 else tuple(range(sec))


def prepare_kernel(depth, basis_hbm, site_hbm, integrals_ref, *refs):
    high_ref, low_ref, part_ref, row_ref = refs[:4]
    scratch = refs[4:]
    row_ref[...] = integrals_ref[...]
    basis_ref, site_ref, basis_sem, site_sem = scratch
    _, sites, old, cols = basis_ref.shape
    rows = part_ref.shape[3]
    me = lax.axis_index("sec")
    site_copy = pltpu.make_async_copy(site_hbm, site_ref, site_sem)
    site_copy.start()
    copies = [
        (part, site, pltpu.make_async_copy(
            basis_hbm.at[part, site], basis_ref.at[part, site], basis_sem.at[part, site]
        ))
        for part in range(2)
        for site in range(sites)
    ]
    for _, _, copy in copies:
        copy.start()
    for part, site, copy in copies:
        copy.wait()
        for step, far in enumerate(order(old // depth)):
            start = pl.multiple_of((me ^ far) * depth, depth)
            at = pl.ds((step * 2 + part) * depth, depth)
            high, low = split(basis_ref[part, site, pl.ds(start, depth), :])
            high_ref[at, pl.ds(site * cols, cols)] = high
            low_ref[at, pl.ds(site * cols, cols)] = low
    site_copy.wait()
    for comp in range(part_ref.shape[1]):
        for site in range(sites):
            real = imag = None
            for other in range(sites):
                sr, si = site_ref[0, comp, site, other], site_ref[1, comp, site, other]
                br, bi = basis_ref[0, other, :rows, :], basis_ref[1, other, :rows, :]
                tr, ti = sr * br - si * bi, sr * bi + si * br
                real = tr if real is None else real + tr
                imag = ti if imag is None else imag + ti
            part_ref[0, comp, site] = real
            part_ref[1, comp, site] = imag


def prepare(basis, site_terms, integrals, rows, depth):
    _, sites, old, cols = basis.shape
    comps = site_terms.shape[1]
    half = jax.ShapeDtypeStruct((2 * old, sites * cols), jnp.bfloat16)
    part = jax.ShapeDtypeStruct((2, comps, sites, rows, cols), jnp.float32)
    return call(
        functools.partial(prepare_kernel, depth),
        (half, half, part, jax.ShapeDtypeStruct(integrals.shape, integrals.dtype)),
        [HBM, HBM, VMEM],
        8 * comps * sites * sites * rows * cols,
        [
            pltpu.VMEM(basis.shape, basis.dtype),
            pltpu.SMEM(site_terms.shape, site_terms.dtype),
            pltpu.SemaphoreType.DMA((2, sites)),
            pltpu.SemaphoreType.DMA,
        ],
    )(basis, site_terms, integrals)


def pack(block, tables):
    _, per, rows, cols = block.shape

    def kernel(block_ref, *refs):
        out_ref = refs[-1]
        out_ref[:, :, :rows, :] = block_ref[...]
        out_ref[:, :, rows:, :] = jnp.zeros((2, per) + TILE, jnp.float32)
        for under, ref in enumerate(refs[:-1]):
            _, comps, norms = ref.shape
            for part in range(2):
                first = rows + part * comps
                out_ref[under, 0, first : first + comps, :norms] = ref[part]

    out = jax.ShapeDtypeStruct((2, per, rows + TILE[0], cols), block.dtype)
    return call(kernel, out, [VMEM] * (1 + len(tables)), 0)(block, *tables)


def after(x, *others):
    def kernel(x_ref, *refs):
        refs[-1][...] = x_ref[...]

    out = jax.ShapeDtypeStruct(x.shape, x.dtype)
    return call(kernel, out, [VMEM] + [ANY] * len(others), 0)(x, *others)


def renorm_kernel(steps, parts, carried, awaited, streamed, *refs):
    count = sum(parts)
    high_ref, low_ref = refs[count : count + 2]
    first = count + 2 + carried + awaited
    out_ref, left_high, left_low = refs[first : first + 3]
    out_hbm, out_ref, sems = (out_ref,) + refs[-2:] if streamed else (None, out_ref, None)
    _, ops, sites, rows, cols = out_ref.shape
    depth = refs[0].shape[-1]
    tall = ops * rows
    for step in range(len(steps)):
        first = sum(parts[:step])
        value = sum(refs[at][:, :, :rows, :] for at in range(first + 1, first + parts[step]))
        value = (refs[first][:, :, :rows, :] + value).reshape(2, tall, depth)
        for scratch, real, imag in zip((left_high, left_low), split(value[0]), split(value[1])):
            at = 2 * step * depth
            scratch[:tall, at : at + depth] = real
            scratch[:tall, at + depth : at + 2 * depth] = -imag
            scratch[tall:, at : at + depth] = imag
            scratch[tall:, at + depth : at + 2 * depth] = real
    dot = functools.partial(jnp.dot, preferred_element_type=jnp.float32)
    deep = slice(2 * depth * steps[0], 2 * depth * (steps[-1] + 1))
    copies = []
    for first in range(0, sites * cols, WIDE):
        at = (deep, slice(first, first + WIDE))
        total = dot(left_high[...], high_ref[at])
        total = total + dot(left_high[...], low_ref[at])
        total = total + dot(left_low[...], high_ref[at])
        some = range(first // cols, (first + WIDE) // cols)
        for part in range(2):
            for op in range(ops):
                for site in some:
                    across = slice(site * cols - first, site * cols - first + cols)
                    start = part * tall + op * rows
                    value = total[start : start + rows, across]
                    if carried:
                        value = value + refs[count + 2][part, op, site]
                    out_ref[part, op, site] = value
                if streamed:
                    piece = (part, op, pl.ds(some.start, len(some)))
                    copies.append(
                        pltpu.make_async_copy(
                            out_ref.at[piece], out_hbm.at[piece], sems.at[len(copies)]
                        )
                    )
                    copies[-1].start()
    for copy in copies:
        copy.wait()


def renorm(blocks, steps, high, low, carry, shape, streamed=False, awaited=()):
    blocks = [block if isinstance(block, tuple) else (block,) for block in blocks]
    blocks = blocks[steps.start : steps.stop]
    parts = tuple(len(block) for block in blocks)
    args = sum(blocks, ()) + (high, low) + (() if carry is None else (carry,))
    _, ops, sites, rows, cols = shape
    depth = blocks[0][0].shape[-1]
    left = pltpu.VMEM((2 * ops * rows, 2 * depth * len(blocks)), jnp.bfloat16)
    pieces = 2 * ops * sites * cols // WIDE
    held = [pltpu.VMEM(shape, jnp.float32), pltpu.SemaphoreType.DMA((pieces,))]
    return pl.pallas_call(
        functools.partial(
            renorm_kernel, steps, parts, carry is not None, len(awaited), streamed
        ),
        out_shape=jax.ShapeDtypeStruct(shape, jnp.float32),
        in_specs=[VMEM] * len(args) + [ANY] * len(awaited),
        out_specs=HBM if streamed else VMEM,
        scratch_shapes=[left, left] + (held if streamed else []),
        cost_estimate=pl.CostEstimate(
            flops=24 * ops * rows * depth * len(blocks) * sites * cols,
            bytes_accessed=4 << 20,
            transcendentals=0,
        ),
        compiler_params=pltpu.CompilerParams(vmem_limit_bytes=VMEM_BYTES),
    )(*args, *awaited)


def total(parts, awaited):
    def kernel(*refs):
        refs[-1][...] = sum((ref[...] for ref in refs[1 : len(parts)]), refs[0][...])

    out = jax.ShapeDtypeStruct(parts[0].shape, parts[0].dtype)
    specs = [VMEM] * len(parts) + [ANY] * len(awaited)
    return call(kernel, out, specs, out.size * len(parts))(*parts, *awaited)


def combine_kernel(operators, tables, per, *refs):
    outs = refs[len(refs) - len(tables) :]
    comps, rows, _ = outs[0].shape[1:]
    me = lax.axis_index("pair")
    for (held, under), out_ref in zip(tables, outs):
        lane = lax.broadcasted_iota(jnp.int32, (1, refs[held].shape[-1]), 1)
        for comp in range(comps):
            real = imag = None
            for array, place, op, key in operators:
                coefficients = []
                for part in range(2):
                    at = part * comps + comp
                    if under is None:
                        row = refs[held][part, comp : comp + 1, :]
                    else:
                        row = refs[held][under, 0, rows + at : rows + at + 1, :]
                    here = jnp.where(lane == (me ^ key) * per + op, row, 0.0)
                    coefficients.append(jnp.sum(here, axis=1, keepdims=True))
                cr, ci = coefficients
                br, bi = (refs[array][part, place, :rows, :] for part in range(2))
                tr, ti = cr * br - ci * bi, cr * bi + ci * br
                real = tr if real is None else real + tr
                imag = ti if imag is None else imag + ti
            out_ref[0, comp] = real
            out_ref[1, comp] = imag


def combine(arrays, operators, tables, per, shape, awaited=()):
    rows, cols = shape[2:]
    return call(
        functools.partial(combine_kernel, operators, tables, per),
        (jax.ShapeDtypeStruct(shape, jnp.float32),) * len(tables),
        [VMEM] * len(arrays) + [ANY] * len(awaited),
        8 * len(tables) * len(operators) * rows * cols,
    )(*arrays, *awaited)


def swap(x, axis, size, key):
    return lax.ppermute(x, axis, [(at, at ^ key) for at in range(size)])


def chip_blocks(own, row, beside, pairs):
    per = own.shape[1]
    arrays, tables = [own], []
    operators = [(0, op, op, 0) for op in range(per)]
    if pairs == 8:
        for key in (2, 4):
            operators += [(len(arrays), op, op, key) for op in range(per)]
            arrays.append(swap(own, "pair", pairs, key))
        operators += [(3, op, op, 6) for op in range(per)]
        arrays += [
            swap(pack(arrays[1], [row, beside]), "pair", pairs, 4),
            row,
            beside,
        ]
        tables = [(4, None), (5, None), (3, 0), (3, 1)]
    else:
        arrays[0] = pack(own, [row])
        tables = [(0, 0)]
        for key in range(2, pairs, 2):
            operators += [(len(arrays), op, op, key) for op in range(per)]
            tables.append((len(arrays), 0))
            arrays.append(swap(arrays[0], "pair", pairs, key))
    return arrays, operators, tables


def on_device(pairs, sec, normal_ops, integrals, site_terms, basis):
    _, norms, rows, depth = normal_ops.shape
    _, sites, _, cols = basis.shape
    comps = integrals.shape[1]
    shape = (2, comps, rows, depth)
    two = swap(normal_ops, "sec", sec, 2)
    one = swap(normal_ops, "sec", sec, 1)
    beside = swap(integrals, "pair", pairs, 2)
    sibling = swap(integrals, "pair", pairs, 1)
    high, low, site_part, row = prepare(basis, site_terms, integrals, rows, depth)
    arrays, operators, tables = chip_blocks(normal_ops, row, beside, pairs)
    two = after(two, sibling)
    three = swap(two, "sec", sec, 1)
    two = after(after(two, arrays[2]), one)
    normals = [three, one, normal_ops, two]
    held = arrays + [row, sibling]
    here = [(len(arrays), None), (len(arrays) + 1, None)]
    mine, other = combine(held, operators, here, norms, shape)
    held = [two, swap(two, "pair", pairs, 1)] + arrays
    operators = [(key, op, op, key) for key in range(2) for op in range(norms)]
    tables = [(2 + at, part) for at, part in tables]
    parts = combine(held, operators, tables, norms, shape)
    comp_ops = total([mine, swap(other, "pair", pairs, 1)], [parts[0]])
    far = swap(comp_ops, "sec", sec, 3)
    near = swap(comp_ops, "sec", sec, 1)
    last = pairs // 2
    arrived = {
        key: swap(parts[key // 2], "pair", pairs, key)
        for key in range(2, pairs, 2)
        if key != last
    }
    most = total([parts[0]] + list(arrived.values()), [])
    rest = swap(after(parts[last // 2], comp_ops, arrived[2]), "pair", pairs, last)
    shape = (2, norms, sites, rows, cols)
    early = renorm(normals, range(1, sec), high, low, None, shape)
    new_normal = renorm(normals, range(1), high, low, early, shape, True)
    shape = (2, comps, sites, rows, cols)
    arrived = [far, near, comp_ops, (most, rest)]
    early = renorm(arrived, range(2, 3), high, low, site_part, shape, awaited=[most])
    early = renorm(arrived, range(2), high, low, early, shape)
    return new_normal, renorm(arrived, range(3, sec), high, low, early, shape, True)


def solution(mesh):
    placed = (
        P(None, "pair", None, "sec"),
        P(None, "pair", None),
        P(None, "pair", None, None),
        P(None, None, None, "sec"),
    )
    return jax.shard_map(
        functools.partial(on_device, mesh.shape["pair"], mesh.shape["sec"]),
        mesh=mesh,
        in_specs=placed,
        out_specs=(P(None, "pair", None, None, "sec"), P(None, "pair", None, None, "sec")),
        check_vma=False,
    )
```

```python
import functools

import jax
import jax.numpy as jnp
from jax import lax
from jax.experimental import pallas as pl
from jax.experimental.pallas import tpu as pltpu
from jax.sharding import PartitionSpec as P

VMEM_BYTES = 24 * 1024 * 1024
WIDE = 256
TILE = (8, 128)
VMEM = pl.BlockSpec(memory_space=pltpu.VMEM)
ANY = pl.BlockSpec(memory_space=pl.ANY)
HBM = pl.BlockSpec(memory_space=pltpu.HBM)


def call(kernel, out_shape, in_specs, flops, scratch_shapes=(), moved=4 << 20):
    return pl.pallas_call(
        kernel,
        out_shape=out_shape,
        in_specs=in_specs,
        out_specs=jax.tree.map(lambda _: VMEM, out_shape),
        scratch_shapes=scratch_shapes,
        cost_estimate=pl.CostEstimate(flops=flops, bytes_accessed=moved, transcendentals=0),
        compiler_params=pltpu.CompilerParams(vmem_limit_bytes=VMEM_BYTES),
    )


def split(x):
    high = x.astype(jnp.bfloat16)
    return high, (x - high.astype(jnp.float32)).astype(jnp.bfloat16)


def order(sec):
    return (3, 0, 1, 2) if sec == 4 else tuple(range(sec))


def prepare_kernel(depth, basis_hbm, site_hbm, integrals_ref, *refs):
    high_ref, low_ref, part_ref, row_ref = refs[:4]
    scratch = refs[4:]
    row_ref[...] = integrals_ref[...]
    basis_ref, site_ref, basis_sem, site_sem = scratch
    _, sites, old, cols = basis_ref.shape
    rows = part_ref.shape[3]
    me = lax.axis_index("sec")
    site_copy = pltpu.make_async_copy(site_hbm, site_ref, site_sem)
    site_copy.start()
    copies = [
        (part, site, pltpu.make_async_copy(
            basis_hbm.at[part, site], basis_ref.at[part, site], basis_sem.at[part, site]
        ))
        for part in range(2)
        for site in range(sites)
    ]
    for _, _, copy in copies:
        copy.start()
    for part, site, copy in copies:
        copy.wait()
        for step, far in enumerate(order(old // depth)):
            start = pl.multiple_of((me ^ far) * depth, depth)
            at = pl.ds((step * 2 + part) * depth, depth)
            high, low = split(basis_ref[part, site, pl.ds(start, depth), :])
            high_ref[at, pl.ds(site * cols, cols)] = high
            low_ref[at, pl.ds(site * cols, cols)] = low
    site_copy.wait()
    for comp in range(part_ref.shape[1]):
        for site in range(sites):
            real = imag = None
            for other in range(sites):
                sr, si = site_ref[0, comp, site, other], site_ref[1, comp, site, other]
                br, bi = basis_ref[0, other, :rows, :], basis_ref[1, other, :rows, :]
                tr, ti = sr * br - si * bi, sr * bi + si * br
                real = tr if real is None else real + tr
                imag = ti if imag is None else imag + ti
            part_ref[0, comp, site] = real
            part_ref[1, comp, site] = imag


def prepare(basis, site_terms, integrals, rows, depth):
    _, sites, old, cols = basis.shape
    comps = site_terms.shape[1]
    half = jax.ShapeDtypeStruct((2 * old, sites * cols), jnp.bfloat16)
    part = jax.ShapeDtypeStruct((2, comps, sites, rows, cols), jnp.float32)
    return call(
        functools.partial(prepare_kernel, depth),
        (half, half, part, jax.ShapeDtypeStruct(integrals.shape, integrals.dtype)),
        [HBM, HBM, VMEM],
        8 * comps * sites * sites * rows * cols,
        [
            pltpu.VMEM(basis.shape, basis.dtype),
            pltpu.SMEM(site_terms.shape, site_terms.dtype),
            pltpu.SemaphoreType.DMA((2, sites)),
            pltpu.SemaphoreType.DMA,
        ],
        4 << 20,
    )(basis, site_terms, integrals)


def pack(block, tables):
    _, per, rows, cols = block.shape

    def kernel(block_ref, *refs):
        out_ref = refs[-1]
        out_ref[:, :, :rows, :] = block_ref[...]
        out_ref[:, :, rows:, :] = jnp.zeros((2, per) + TILE, jnp.float32)
        for under, ref in enumerate(refs[:-1]):
            _, comps, norms = ref.shape
            for part in range(2):
                first = rows + part * comps
                out_ref[under, 0, first : first + comps, :norms] = ref[part]

    out = jax.ShapeDtypeStruct((2, per, rows + TILE[0], cols), block.dtype)
    return call(kernel, out, [VMEM] * (1 + len(tables)), 0)(block, *tables)


def after(x, *others):
    def kernel(x_ref, *refs):
        refs[-1][...] = x_ref[...]

    out = jax.ShapeDtypeStruct(x.shape, x.dtype)
    return call(kernel, out, [VMEM] + [ANY] * len(others), 0)(x, *others)


def renorm_kernel(steps, parts, carried, awaited, streamed, *refs):
    count = sum(parts)
    high_ref, low_ref = refs[count : count + 2]
    first = count + 2 + carried + awaited
    out_ref, left_high, left_low = refs[first : first + 3]
    out_hbm, out_ref, sems = (out_ref,) + refs[-2:] if streamed else (None, out_ref, None)
    _, ops, sites, rows, cols = out_ref.shape
    depth = refs[0].shape[-1]
    tall = ops * rows
    for step in range(len(steps)):
        first = sum(parts[:step])
        value = sum(refs[at][:, :, :rows, :] for at in range(first + 1, first + parts[step]))
        value = (refs[first][:, :, :rows, :] + value).reshape(2, tall, depth)
        for scratch, real, imag in zip((left_high, left_low), split(value[0]), split(value[1])):
            at = 2 * step * depth
            scratch[:tall, at : at + depth] = real
            scratch[:tall, at + depth : at + 2 * depth] = -imag
            scratch[tall:, at : at + depth] = imag
            scratch[tall:, at + depth : at + 2 * depth] = real
    dot = functools.partial(jnp.dot, preferred_element_type=jnp.float32)
    deep = slice(2 * depth * steps[0], 2 * depth * (steps[-1] + 1))
    copies = []
    for first in range(0, sites * cols, WIDE):
        at = (deep, slice(first, first + WIDE))
        total = dot(left_high[...], high_ref[at])
        total = total + dot(left_high[...], low_ref[at])
        total = total + dot(left_low[...], high_ref[at])
        some = range(first // cols, (first + WIDE) // cols)
        for part in range(2):
            for op in range(ops):
                for site in some:
                    across = slice(site * cols - first, site * cols - first + cols)
                    start = part * tall + op * rows
                    value = total[start : start + rows, across]
                    if carried:
                        value = value + refs[count + 2][part, op, site]
                    out_ref[part, op, site] = value
                if streamed:
                    piece = (part, op, pl.ds(some.start, len(some)))
                    copies.append(
                        pltpu.make_async_copy(
                            out_ref.at[piece], out_hbm.at[piece], sems.at[len(copies)]
                        )
                    )
                    copies[-1].start()
    for copy in copies:
        copy.wait()


def renorm(blocks, steps, high, low, carry, shape, streamed=False, awaited=()):
    blocks = [block if isinstance(block, tuple) else (block,) for block in blocks]
    blocks = blocks[steps.start : steps.stop]
    parts = tuple(len(block) for block in blocks)
    args = sum(blocks, ()) + (high, low) + (() if carry is None else (carry,))
    _, ops, sites, rows, cols = shape
    depth = blocks[0][0].shape[-1]
    left = pltpu.VMEM((2 * ops * rows, 2 * depth * len(blocks)), jnp.bfloat16)
    pieces = 2 * ops * sites * cols // WIDE
    held = [pltpu.VMEM(shape, jnp.float32), pltpu.SemaphoreType.DMA((pieces,))]
    return pl.pallas_call(
        functools.partial(
            renorm_kernel, steps, parts, carry is not None, len(awaited), streamed
        ),
        out_shape=jax.ShapeDtypeStruct(shape, jnp.float32),
        in_specs=[VMEM] * len(args) + [ANY] * len(awaited),
        out_specs=HBM if streamed else VMEM,
        scratch_shapes=[left, left] + (held if streamed else []),
        cost_estimate=pl.CostEstimate(
            flops=24 * ops * rows * depth * len(blocks) * sites * cols,
            bytes_accessed=4 << 20,
            transcendentals=0,
        ),
        compiler_params=pltpu.CompilerParams(vmem_limit_bytes=VMEM_BYTES),
    )(*args, *awaited)


def total(parts, awaited):
    def kernel(*refs):
        refs[-1][...] = sum((ref[...] for ref in refs[1 : len(parts)]), refs[0][...])

    out = jax.ShapeDtypeStruct(parts[0].shape, parts[0].dtype)
    specs = [VMEM] * len(parts) + [ANY] * len(awaited)
    return call(kernel, out, specs, out.size * len(parts))(*parts, *awaited)


def combine_kernel(operators, tables, per, *refs):
    outs = refs[len(refs) - len(tables) :]
    comps, rows, _ = outs[0].shape[1:]
    me = lax.axis_index("pair")
    for (held, under), out_ref in zip(tables, outs):
        lane = lax.broadcasted_iota(jnp.int32, (1, refs[held].shape[-1]), 1)
        for comp in range(comps):
            real = imag = None
            for array, place, op, key in operators:
                coefficients = []
                for part in range(2):
                    at = part * comps + comp
                    if under is None:
                        row = refs[held][part, comp : comp + 1, :]
                    else:
                        row = refs[held][under, 0, rows + at : rows + at + 1, :]
                    here = jnp.where(lane == (me ^ key) * per + op, row, 0.0)
                    coefficients.append(jnp.sum(here, axis=1, keepdims=True))
                cr, ci = coefficients
                br, bi = (refs[array][part, place, :rows, :] for part in range(2))
                tr, ti = cr * br - ci * bi, cr * bi + ci * br
                real = tr if real is None else real + tr
                imag = ti if imag is None else imag + ti
            out_ref[0, comp] = real
            out_ref[1, comp] = imag


def combine(arrays, operators, tables, per, shape, awaited=()):
    rows, cols = shape[2:]
    return call(
        functools.partial(combine_kernel, operators, tables, per),
        (jax.ShapeDtypeStruct(shape, jnp.float32),) * len(tables),
        [VMEM] * len(arrays) + [ANY] * len(awaited),
        8 * len(tables) * len(operators) * rows * cols,
        moved=4 << 20,
    )(*arrays, *awaited)


def swap(x, axis, size, key):
    return lax.ppermute(x, axis, [(at, at ^ key) for at in range(size)])


def chip_blocks(own, row, beside, pairs):
    per = own.shape[1]
    arrays, tables = [own], []
    operators = [(0, op, op, 0) for op in range(per)]
    if pairs == 8:
        for key in (2, 4):
            operators += [(len(arrays), op, op, key) for op in range(per)]
            arrays.append(swap(own, "pair", pairs, key))
        operators += [(3, op, op, 6) for op in range(per)]
        arrays += [
            swap(pack(arrays[1], [row, beside]), "pair", pairs, 4),
            row,
            beside,
        ]
        tables = [(4, None), (5, None), (3, 0), (3, 1)]
    else:
        arrays[0] = pack(own, [row])
        tables = [(0, 0)]
        for key in range(2, pairs, 2):
            operators += [(len(arrays), op, op, key) for op in range(per)]
            tables.append((len(arrays), 0))
            arrays.append(swap(arrays[0], "pair", pairs, key))
    return arrays, operators, tables


def on_device(pairs, sec, normal_ops, integrals, site_terms, basis):
    _, norms, rows, depth = normal_ops.shape
    _, sites, _, cols = basis.shape
    comps = integrals.shape[1]
    shape = (2, comps, rows, depth)
    two = swap(normal_ops, "sec", sec, 2)
    one = swap(normal_ops, "sec", sec, 1)
    beside = swap(integrals, "pair", pairs, 2)
    sibling = swap(integrals, "pair", pairs, 1)
    high, low, site_part, row = prepare(basis, site_terms, integrals, rows, depth)
    arrays, operators, tables = chip_blocks(normal_ops, row, beside, pairs)
    two = after(two, sibling)
    three = swap(two, "sec", sec, 1)
    two = after(after(two, arrays[2]), one)
    normals = [three, normal_ops, one, two]
    held = arrays + [row, sibling]
    here = [(len(arrays), None), (len(arrays) + 1, None)]
    mine, other = combine(held, operators, here, norms, shape)
    held = [two, swap(two, "pair", pairs, 1)] + arrays
    operators = [(key, op, op, key) for key in range(2) for op in range(norms)]
    tables = [(2 + at, part) for at, part in tables]
    parts = combine(held, operators, tables, norms, shape)
    comp_ops = total([mine, swap(other, "pair", pairs, 1)], [parts[0]])
    far = swap(comp_ops, "sec", sec, 3)
    near = swap(comp_ops, "sec", sec, 1)
    last = pairs // 2
    arrived = {
        key: swap(parts[key // 2], "pair", pairs, key)
        for key in range(2, pairs, 2)
        if key != last
    }
    most = total([parts[0]] + list(arrived.values()), [])
    rest = swap(after(parts[last // 2], comp_ops, arrived[2]), "pair", pairs, last)
    shape = (2, norms, sites, rows, cols)
    early = renorm(normals, range(1, sec), high, low, None, shape)
    new_normal = renorm(normals, range(1), high, low, early, shape, True)
    shape = (2, comps, sites, rows, cols)
    arrived = [far, comp_ops, near, (most, rest)]
    early = renorm(arrived, range(2), high, low, site_part, shape, awaited=[most])
    return new_normal, renorm(arrived, range(2, sec), high, low, early, shape, True)


def solution(mesh):
    placed = (
        P(None, "pair", None, "sec"),
        P(None, "pair", None),
        P(None, "pair", None, None),
        P(None, None, None, "sec"),
    )
    return jax.shard_map(
        functools.partial(on_device, mesh.shape["pair"], mesh.shape["sec"]),
        mesh=mesh,
        in_specs=placed,
        out_specs=(P(None, "pair", None, None, "sec"), P(None, "pair", None, None, "sec")),
        check_vma=False,
    )
```

```python
import functools

import jax
import jax.numpy as jnp
from jax import lax
from jax.experimental import pallas as pl
from jax.experimental.pallas import tpu as pltpu
from jax.sharding import PartitionSpec as P

VMEM_BYTES = 24 * 1024 * 1024
WIDE = 256
TILE = (8, 128)
VMEM = pl.BlockSpec(memory_space=pltpu.VMEM)
ANY = pl.BlockSpec(memory_space=pl.ANY)
HBM = pl.BlockSpec(memory_space=pltpu.HBM)


def call(kernel, out_shape, in_specs, flops, scratch_shapes=(), moved=4 << 20):
    return pl.pallas_call(
        kernel,
        out_shape=out_shape,
        in_specs=in_specs,
        out_specs=jax.tree.map(lambda _: VMEM, out_shape),
        scratch_shapes=scratch_shapes,
        cost_estimate=pl.CostEstimate(flops=flops, bytes_accessed=moved, transcendentals=0),
        compiler_params=pltpu.CompilerParams(vmem_limit_bytes=VMEM_BYTES),
    )


def split(x):
    high = x.astype(jnp.bfloat16)
    return high, (x - high.astype(jnp.float32)).astype(jnp.bfloat16)


def order(sec):
    return (3, 0, 1, 2) if sec == 4 else tuple(range(sec))


def prepare_kernel(depth, basis_hbm, site_hbm, integrals_ref, *refs):
    split_ref, part_ref, row_ref = refs[:3]
    scratch = refs[3:]
    row_ref[...] = integrals_ref[...]
    basis_ref, site_ref, basis_sem, site_sem = scratch
    _, sites, old, cols = basis_ref.shape
    rows = part_ref.shape[3]
    me = lax.axis_index("sec")
    site_copy = pltpu.make_async_copy(site_hbm, site_ref, site_sem)
    site_copy.start()
    copies = [
        (part, site, pltpu.make_async_copy(
            basis_hbm.at[part, site], basis_ref.at[part, site], basis_sem.at[part, site]
        ))
        for part in range(2)
        for site in range(sites)
    ]
    for _, _, copy in copies:
        copy.start()
    for part, site, copy in copies:
        copy.wait()
        for step, far in enumerate(order(old // depth)):
            start = pl.multiple_of((me ^ far) * depth, depth)
            high, low = split(basis_ref[part, site, pl.ds(start, depth), :])
            for which, value in enumerate((high, low, high)):
                at = pl.ds(((step * 3 + which) * 2 + part) * depth, depth)
                split_ref[at, pl.ds(site * cols, cols)] = value
    site_copy.wait()
    for comp in range(part_ref.shape[1]):
        for site in range(sites):
            real = imag = None
            for other in range(sites):
                sr, si = site_ref[0, comp, site, other], site_ref[1, comp, site, other]
                br, bi = basis_ref[0, other, :rows, :], basis_ref[1, other, :rows, :]
                tr, ti = sr * br - si * bi, sr * bi + si * br
                real = tr if real is None else real + tr
                imag = ti if imag is None else imag + ti
            part_ref[0, comp, site] = real
            part_ref[1, comp, site] = imag


def prepare(basis, site_terms, integrals, rows, depth):
    _, sites, old, cols = basis.shape
    comps = site_terms.shape[1]
    halves = jax.ShapeDtypeStruct((6 * old, sites * cols), jnp.bfloat16)
    part = jax.ShapeDtypeStruct((2, comps, sites, rows, cols), jnp.float32)
    return call(
        functools.partial(prepare_kernel, depth),
        (halves, part, jax.ShapeDtypeStruct(integrals.shape, integrals.dtype)),
        [HBM, HBM, VMEM],
        8 * comps * sites * sites * rows * cols,
        [
            pltpu.VMEM(basis.shape, basis.dtype),
            pltpu.SMEM(site_terms.shape, site_terms.dtype),
            pltpu.SemaphoreType.DMA((2, sites)),
            pltpu.SemaphoreType.DMA,
        ],
        4 << 20,
    )(basis, site_terms, integrals)


def pack(block, tables):
    _, per, rows, cols = block.shape

    def kernel(block_ref, *refs):
        out_ref = refs[-1]
        out_ref[:, :, :rows, :] = block_ref[...]
        out_ref[:, :, rows:, :] = jnp.zeros((2, per) + TILE, jnp.float32)
        for under, ref in enumerate(refs[:-1]):
            _, comps, norms = ref.shape
            for part in range(2):
                first = rows + part * comps
                out_ref[under, 0, first : first + comps, :norms] = ref[part]

    out = jax.ShapeDtypeStruct((2, per, rows + TILE[0], cols), block.dtype)
    return call(kernel, out, [VMEM] * (1 + len(tables)), 0)(block, *tables)


def after(x, *others):
    def kernel(x_ref, *refs):
        refs[-1][...] = x_ref[...]

    out = jax.ShapeDtypeStruct(x.shape, x.dtype)
    return call(kernel, out, [VMEM] + [ANY] * len(others), 0)(x, *others)


def renorm_kernel(steps, parts, carried, awaited, streamed, *refs):
    count = sum(parts)
    split_ref = refs[count]
    first = count + 1 + carried + awaited
    out_ref, left = refs[first : first + 2]
    out_hbm, out_ref, sems = (out_ref,) + refs[-2:] if streamed else (None, out_ref, None)
    _, ops, sites, rows, cols = out_ref.shape
    depth = refs[0].shape[-1]
    tall = ops * rows
    for step in range(len(steps)):
        first = sum(parts[:step])
        value = sum(refs[at][:, :, :rows, :] for at in range(first + 1, first + parts[step]))
        value = (refs[first][:, :, :rows, :] + value).reshape(2, tall, depth)
        (rh, rl), (ih, il) = split(value[0]), split(value[1])
        for which, (real, imag) in enumerate(((rh, ih), (rh, ih), (rl, il))):
            at = 2 * (step * 3 + which) * depth
            left[:tall, at : at + depth] = real
            left[:tall, at + depth : at + 2 * depth] = -imag
            left[tall:, at : at + depth] = imag
            left[tall:, at + depth : at + 2 * depth] = real
    deep = slice(6 * depth * steps[0], 6 * depth * (steps[-1] + 1))
    copies = []
    for first in range(0, sites * cols, WIDE):
        at = (deep, slice(first, first + WIDE))
        total = jnp.dot(left[...], split_ref[at], preferred_element_type=jnp.float32)
        some = range(first // cols, (first + WIDE) // cols)
        for part in range(2):
            for op in range(ops):
                for site in some:
                    across = slice(site * cols - first, site * cols - first + cols)
                    start = part * tall + op * rows
                    value = total[start : start + rows, across]
                    if carried:
                        value = value + refs[count + 1][part, op, site]
                    out_ref[part, op, site] = value
                if streamed:
                    piece = (part, op, pl.ds(some.start, len(some)))
                    copies.append(
                        pltpu.make_async_copy(
                            out_ref.at[piece], out_hbm.at[piece], sems.at[len(copies)]
                        )
                    )
                    copies[-1].start()
    for copy in copies:
        copy.wait()


def renorm(blocks, steps, basis, carry, shape, streamed=False, awaited=()):
    blocks = [block if isinstance(block, tuple) else (block,) for block in blocks]
    blocks = blocks[steps.start : steps.stop]
    parts = tuple(len(block) for block in blocks)
    args = sum(blocks, ()) + (basis,) + (() if carry is None else (carry,))
    _, ops, sites, rows, cols = shape
    depth = blocks[0][0].shape[-1]
    left = pltpu.VMEM((2 * ops * rows, 6 * depth * len(blocks)), jnp.bfloat16)
    pieces = 2 * ops * sites * cols // WIDE
    held = [pltpu.VMEM(shape, jnp.float32), pltpu.SemaphoreType.DMA((pieces,))]
    return pl.pallas_call(
        functools.partial(
            renorm_kernel, steps, parts, carry is not None, len(awaited), streamed
        ),
        out_shape=jax.ShapeDtypeStruct(shape, jnp.float32),
        in_specs=[VMEM] * len(args) + [ANY] * len(awaited),
        out_specs=HBM if streamed else VMEM,
        scratch_shapes=[left] + (held if streamed else []),
        cost_estimate=pl.CostEstimate(
            flops=24 * ops * rows * depth * len(blocks) * sites * cols,
            bytes_accessed=4 << 20,
            transcendentals=0,
        ),
        compiler_params=pltpu.CompilerParams(vmem_limit_bytes=VMEM_BYTES),
    )(*args, *awaited)


def total(parts, awaited):
    def kernel(*refs):
        refs[-1][...] = sum((ref[...] for ref in refs[1 : len(parts)]), refs[0][...])

    out = jax.ShapeDtypeStruct(parts[0].shape, parts[0].dtype)
    specs = [VMEM] * len(parts) + [ANY] * len(awaited)
    return call(kernel, out, specs, out.size * len(parts))(*parts, *awaited)


def combine_kernel(operators, tables, per, *refs):
    outs = refs[len(refs) - len(tables) :]
    comps, rows, _ = outs[0].shape[1:]
    me = lax.axis_index("pair")
    for (held, under), out_ref in zip(tables, outs):
        lane = lax.broadcasted_iota(jnp.int32, (1, refs[held].shape[-1]), 1)
        for comp in range(comps):
            real = imag = None
            for array, place, op, key in operators:
                coefficients = []
                for part in range(2):
                    at = part * comps + comp
                    if under is None:
                        row = refs[held][part, comp : comp + 1, :]
                    else:
                        row = refs[held][under, 0, rows + at : rows + at + 1, :]
                    here = jnp.where(lane == (me ^ key) * per + op, row, 0.0)
                    coefficients.append(jnp.sum(here, axis=1, keepdims=True))
                cr, ci = coefficients
                br, bi = (refs[array][part, place, :rows, :] for part in range(2))
                tr, ti = cr * br - ci * bi, cr * bi + ci * br
                real = tr if real is None else real + tr
                imag = ti if imag is None else imag + ti
            out_ref[0, comp] = real
            out_ref[1, comp] = imag


def combine(arrays, operators, tables, per, shape, awaited=()):
    rows, cols = shape[2:]
    return call(
        functools.partial(combine_kernel, operators, tables, per),
        (jax.ShapeDtypeStruct(shape, jnp.float32),) * len(tables),
        [VMEM] * len(arrays) + [ANY] * len(awaited),
        8 * len(tables) * len(operators) * rows * cols,
        moved=4 << 20,
    )(*arrays, *awaited)


def swap(x, axis, size, key):
    return lax.ppermute(x, axis, [(at, at ^ key) for at in range(size)])


def chip_blocks(own, row, beside, pairs):
    per = own.shape[1]
    arrays, tables = [own], []
    operators = [(0, op, op, 0) for op in range(per)]
    if pairs == 8:
        for key in (2, 4):
            operators += [(len(arrays), op, op, key) for op in range(per)]
            arrays.append(swap(own, "pair", pairs, key))
        operators += [(3, op, op, 6) for op in range(per)]
        arrays += [
            swap(pack(arrays[1], [row, beside]), "pair", pairs, 4),
            row,
            beside,
        ]
        tables = [(4, None), (5, None), (3, 0), (3, 1)]
    else:
        arrays[0] = pack(own, [row])
        tables = [(0, 0)]
        for key in range(2, pairs, 2):
            operators += [(len(arrays), op, op, key) for op in range(per)]
            tables.append((len(arrays), 0))
            arrays.append(swap(arrays[0], "pair", pairs, key))
    return arrays, operators, tables


def on_device(pairs, sec, normal_ops, integrals, site_terms, basis):
    _, norms, rows, depth = normal_ops.shape
    _, sites, _, cols = basis.shape
    comps = integrals.shape[1]
    shape = (2, comps, rows, depth)
    two = swap(normal_ops, "sec", sec, 2)
    one = swap(normal_ops, "sec", sec, 1)
    beside = swap(integrals, "pair", pairs, 2)
    sibling = swap(integrals, "pair", pairs, 1)
    basis_split, site_part, row = prepare(basis, site_terms, integrals, rows, depth)
    arrays, operators, tables = chip_blocks(normal_ops, row, beside, pairs)
    two = after(two, sibling)
    three = swap(two, "sec", sec, 1)
    two = after(after(two, arrays[2]), one)
    normals = [three, normal_ops, one, two]
    held = arrays + [row, sibling]
    here = [(len(arrays), None), (len(arrays) + 1, None)]
    mine, other = combine(held, operators, here, norms, shape)
    held = [two, swap(two, "pair", pairs, 1)] + arrays
    operators = [(key, op, op, key) for key in range(2) for op in range(norms)]
    tables = [(2 + at, part) for at, part in tables]
    parts = combine(held, operators, tables, norms, shape)
    comp_ops = total([mine, swap(other, "pair", pairs, 1)], [parts[0]])
    far = swap(comp_ops, "sec", sec, 3)
    near = swap(comp_ops, "sec", sec, 1)
    last = pairs // 2
    arrived = {
        key: swap(parts[key // 2], "pair", pairs, key)
        for key in range(2, pairs, 2)
        if key != last
    }
    most = total([parts[0]] + list(arrived.values()), [])
    rest = swap(after(parts[last // 2], comp_ops, arrived[2]), "pair", pairs, last)
    shape = (2, norms, sites, rows, cols)
    early = renorm(normals, range(1, sec), basis_split, None, shape)
    new_normal = renorm(normals, range(1), basis_split, early, shape, True)
    shape = (2, comps, sites, rows, cols)
    arrived = [far, comp_ops, near, (most, rest)]
    early = renorm(arrived, range(2), basis_split, site_part, shape, awaited=[most])
    return new_normal, renorm(arrived, range(2, sec), basis_split, early, shape, True)


def solution(mesh):
    placed = (
        P(None, "pair", None, "sec"),
        P(None, "pair", None),
        P(None, "pair", None, None),
        P(None, None, None, "sec"),
    )
    return jax.shard_map(
        functools.partial(on_device, mesh.shape["pair"], mesh.shape["sec"]),
        mesh=mesh,
        in_specs=placed,
        out_specs=(P(None, "pair", None, None, "sec"), P(None, "pair", None, None, "sec")),
        check_vma=False,
    )
```

```python
import functools

import jax
import jax.numpy as jnp
from jax import lax
from jax.experimental import pallas as pl
from jax.experimental.pallas import tpu as pltpu
from jax.sharding import PartitionSpec as P

VMEM_BYTES = 24 * 1024 * 1024
WIDE = 256
TILE = (8, 128)
VMEM = pl.BlockSpec(memory_space=pltpu.VMEM)
ANY = pl.BlockSpec(memory_space=pl.ANY)
HBM = pl.BlockSpec(memory_space=pltpu.HBM)


def call(kernel, out_shape, in_specs, flops, scratch_shapes=(), moved=4 << 20):
    return pl.pallas_call(
        kernel,
        out_shape=out_shape,
        in_specs=in_specs,
        out_specs=jax.tree.map(lambda _: VMEM, out_shape),
        scratch_shapes=scratch_shapes,
        cost_estimate=pl.CostEstimate(flops=flops, bytes_accessed=moved, transcendentals=0),
        compiler_params=pltpu.CompilerParams(vmem_limit_bytes=VMEM_BYTES),
    )


def split(x):
    high = x.astype(jnp.bfloat16)
    return high, (x - high.astype(jnp.float32)).astype(jnp.bfloat16)


def order(sec):
    return (3, 0, 1, 2) if sec == 4 else tuple(range(sec))


def prepare_kernel(depth, basis_hbm, site_hbm, integrals_ref, *refs):
    split_ref, part_ref, row_ref = refs[:3]
    scratch = refs[3:]
    row_ref[...] = integrals_ref[...]
    basis_ref, site_ref, basis_sem, site_sem = scratch
    _, sites, old, cols = basis_ref.shape
    rows = part_ref.shape[3]
    me = lax.axis_index("sec")
    site_copy = pltpu.make_async_copy(site_hbm, site_ref, site_sem)
    site_copy.start()
    copies = [
        (part, site, pltpu.make_async_copy(
            basis_hbm.at[part, site], basis_ref.at[part, site], basis_sem.at[part, site]
        ))
        for part in range(2)
        for site in range(sites)
    ]
    for _, _, copy in copies:
        copy.start()
    for part, site, copy in copies:
        copy.wait()
        for step, far in enumerate(order(old // depth)):
            start = pl.multiple_of((me ^ far) * depth, depth)
            high, low = split(basis_ref[part, site, pl.ds(start, depth), :])
            for which, value in enumerate((high, low, high)):
                at = pl.ds(((step * 3 + which) * 2 + part) * depth, depth)
                split_ref[at, pl.ds(site * cols, cols)] = value
    site_copy.wait()
    for comp in range(part_ref.shape[1]):
        for site in range(sites):
            real = imag = None
            for other in range(sites):
                sr, si = site_ref[0, comp, site, other], site_ref[1, comp, site, other]
                br, bi = basis_ref[0, other, :rows, :], basis_ref[1, other, :rows, :]
                tr, ti = sr * br - si * bi, sr * bi + si * br
                real = tr if real is None else real + tr
                imag = ti if imag is None else imag + ti
            part_ref[0, comp, site] = real
            part_ref[1, comp, site] = imag


def prepare(basis, site_terms, integrals, rows, depth):
    _, sites, old, cols = basis.shape
    comps = site_terms.shape[1]
    halves = jax.ShapeDtypeStruct((6 * old, sites * cols), jnp.bfloat16)
    part = jax.ShapeDtypeStruct((2, comps, sites, rows, cols), jnp.float32)
    return call(
        functools.partial(prepare_kernel, depth),
        (halves, part, jax.ShapeDtypeStruct(integrals.shape, integrals.dtype)),
        [HBM, HBM, VMEM],
        8 * comps * sites * sites * rows * cols,
        [
            pltpu.VMEM(basis.shape, basis.dtype),
            pltpu.SMEM(site_terms.shape, site_terms.dtype),
            pltpu.SemaphoreType.DMA((2, sites)),
            pltpu.SemaphoreType.DMA,
        ],
        4 << 20,
    )(basis, site_terms, integrals)


def pack(block, tables):
    _, per, rows, cols = block.shape

    def kernel(block_ref, *refs):
        out_ref = refs[-1]
        out_ref[:, :, :rows, :] = block_ref[...]
        out_ref[:, :, rows:, :] = jnp.zeros((2, per) + TILE, jnp.float32)
        for under, ref in enumerate(refs[:-1]):
            _, comps, norms = ref.shape
            for part in range(2):
                first = rows + part * comps
                out_ref[under, 0, first : first + comps, :norms] = ref[part]

    out = jax.ShapeDtypeStruct((2, per, rows + TILE[0], cols), block.dtype)
    return call(kernel, out, [VMEM] * (1 + len(tables)), 0)(block, *tables)


def after(x, *others):
    def kernel(x_ref, *refs):
        refs[-1][...] = x_ref[...]

    out = jax.ShapeDtypeStruct(x.shape, x.dtype)
    return call(kernel, out, [VMEM] + [ANY] * len(others), 0)(x, *others)


def renorm_kernel(steps, parts, carried, awaited, streamed, *refs):
    count = sum(parts)
    split_ref = refs[count]
    first = count + 1 + carried + awaited
    out_ref, left = refs[first : first + 2]
    out_hbm, out_ref, sems = (out_ref,) + refs[-2:] if streamed else (None, out_ref, None)
    _, ops, sites, rows, cols = out_ref.shape
    depth = refs[0].shape[-1]
    tall = ops * rows
    for step in range(len(steps)):
        first = sum(parts[:step])
        value = sum(refs[at][:, :, :rows, :] for at in range(first + 1, first + parts[step]))
        value = (refs[first][:, :, :rows, :] + value).reshape(2, tall, depth)
        (rh, rl), (ih, il) = split(value[0]), split(value[1])
        for which, (real, imag) in enumerate(((rh, ih), (rh, ih), (rl, il))):
            at = 2 * (step * 3 + which) * depth
            left[:tall, at : at + depth] = real
            left[:tall, at + depth : at + 2 * depth] = -imag
            left[tall:, at : at + depth] = imag
            left[tall:, at + depth : at + 2 * depth] = real
    deep = slice(6 * depth * steps[0], 6 * depth * (steps[-1] + 1))
    copies = []
    for first in range(0, sites * cols, WIDE):
        at = (deep, slice(first, first + WIDE))
        total = jnp.dot(left[...], split_ref[at], preferred_element_type=jnp.float32)
        some = range(first // cols, (first + WIDE) // cols)
        for part in range(2):
            for op in range(ops):
                for site in some:
                    across = slice(site * cols - first, site * cols - first + cols)
                    start = part * tall + op * rows
                    value = total[start : start + rows, across]
                    if carried:
                        value = value + refs[count + 1][part, op, site]
                    out_ref[part, op, site] = value
                if streamed:
                    piece = (part, op, pl.ds(some.start, len(some)))
                    copies.append(
                        pltpu.make_async_copy(
                            out_ref.at[piece], out_hbm.at[piece], sems.at[len(copies)]
                        )
                    )
                    copies[-1].start()
    for copy in copies:
        copy.wait()


def renorm(blocks, steps, basis, carry, shape, streamed=False, awaited=()):
    blocks = [block if isinstance(block, tuple) else (block,) for block in blocks]
    blocks = blocks[steps.start : steps.stop]
    parts = tuple(len(block) for block in blocks)
    args = sum(blocks, ()) + (basis,) + (() if carry is None else (carry,))
    _, ops, sites, rows, cols = shape
    depth = blocks[0][0].shape[-1]
    left = pltpu.VMEM((2 * ops * rows, 6 * depth * len(blocks)), jnp.bfloat16)
    pieces = 2 * ops * sites * cols // WIDE
    held = [pltpu.VMEM(shape, jnp.float32), pltpu.SemaphoreType.DMA((pieces,))]
    return pl.pallas_call(
        functools.partial(
            renorm_kernel, steps, parts, carry is not None, len(awaited), streamed
        ),
        out_shape=jax.ShapeDtypeStruct(shape, jnp.float32),
        in_specs=[VMEM] * len(args) + [ANY] * len(awaited),
        out_specs=HBM if streamed else VMEM,
        scratch_shapes=[left] + (held if streamed else []),
        cost_estimate=pl.CostEstimate(
            flops=24 * ops * rows * depth * len(blocks) * sites * cols,
            bytes_accessed=4 << 20,
            transcendentals=0,
        ),
        compiler_params=pltpu.CompilerParams(vmem_limit_bytes=VMEM_BYTES),
    )(*args, *awaited)


def total(parts, awaited):
    def kernel(*refs):
        refs[-1][...] = sum((ref[...] for ref in refs[1 : len(parts)]), refs[0][...])

    out = jax.ShapeDtypeStruct(parts[0].shape, parts[0].dtype)
    specs = [VMEM] * len(parts) + [ANY] * len(awaited)
    return call(kernel, out, specs, out.size * len(parts))(*parts, *awaited)


def combine_kernel(operators, tables, per, *refs):
    outs = refs[len(refs) - len(tables) :]
    comps, rows, _ = outs[0].shape[1:]
    me = lax.axis_index("pair")
    for (held, under), out_ref in zip(tables, outs):
        lane = lax.broadcasted_iota(jnp.int32, (1, refs[held].shape[-1]), 1)
        for comp in range(comps):
            real = imag = None
            for array, place, op, key in operators:
                coefficients = []
                for part in range(2):
                    at = part * comps + comp
                    if under is None:
                        row = refs[held][part, comp : comp + 1, :]
                    else:
                        row = refs[held][under, 0, rows + at : rows + at + 1, :]
                    here = jnp.where(lane == (me ^ key) * per + op, row, 0.0)
                    coefficients.append(jnp.sum(here, axis=1, keepdims=True))
                cr, ci = coefficients
                br, bi = (refs[array][part, place, :rows, :] for part in range(2))
                tr, ti = cr * br - ci * bi, cr * bi + ci * br
                real = tr if real is None else real + tr
                imag = ti if imag is None else imag + ti
            out_ref[0, comp] = real
            out_ref[1, comp] = imag


def combine(arrays, operators, tables, per, shape, awaited=()):
    rows, cols = shape[2:]
    return call(
        functools.partial(combine_kernel, operators, tables, per),
        (jax.ShapeDtypeStruct(shape, jnp.float32),) * len(tables),
        [VMEM] * len(arrays) + [ANY] * len(awaited),
        8 * len(tables) * len(operators) * rows * cols,
        moved=4 << 20,
    )(*arrays, *awaited)


def swap(x, axis, size, key):
    return lax.ppermute(x, axis, [(at, at ^ key) for at in range(size)])


def chip_blocks(own, row, beside, pairs):
    per = own.shape[1]
    arrays, tables = [own], []
    operators = [(0, op, op, 0) for op in range(per)]
    if pairs == 8:
        for key in (2, 4):
            operators += [(len(arrays), op, op, key) for op in range(per)]
            arrays.append(swap(own, "pair", pairs, key))
        operators += [(3, op, op, 6) for op in range(per)]
        arrays += [
            swap(pack(arrays[1], [row, beside]), "pair", pairs, 4),
            row,
            beside,
        ]
        tables = [(4, None), (5, None), (3, 0), (3, 1)]
    else:
        arrays[0] = pack(own, [row])
        tables = [(0, 0)]
        for key in range(2, pairs, 2):
            operators += [(len(arrays), op, op, key) for op in range(per)]
            tables.append((len(arrays), 0))
            arrays.append(swap(arrays[0], "pair", pairs, key))
    return arrays, operators, tables


def on_device(pairs, sec, normal_ops, integrals, site_terms, basis):
    _, norms, rows, depth = normal_ops.shape
    _, sites, _, cols = basis.shape
    comps = integrals.shape[1]
    shape = (2, comps, rows, depth)
    two = swap(normal_ops, "sec", sec, 2)
    one = swap(normal_ops, "sec", sec, 1)
    beside = swap(integrals, "pair", pairs, 2)
    sibling = swap(integrals, "pair", pairs, 1)
    basis_split, site_part, row = prepare(basis, site_terms, integrals, rows, depth)
    arrays, operators, tables = chip_blocks(normal_ops, row, beside, pairs)
    two = after(two, sibling)
    three = swap(two, "sec", sec, 1)
    two = after(after(two, one), arrays[2])
    normals = [three, normal_ops, one, two]
    held = arrays + [row, sibling]
    here = [(len(arrays), None), (len(arrays) + 1, None)]
    mine, other = combine(held, operators, here, norms, shape)
    held = [two, swap(two, "pair", pairs, 1)] + arrays
    operators = [(key, op, op, key) for key in range(2) for op in range(norms)]
    tables = [(2 + at, part) for at, part in tables]
    parts = combine(held, operators, tables, norms, shape)
    comp_ops = total([mine, swap(other, "pair", pairs, 1)], [parts[0]])
    far = swap(comp_ops, "sec", sec, 3)
    near = swap(comp_ops, "sec", sec, 1)
    last = pairs // 2
    arrived = {
        key: swap(parts[key // 2], "pair", pairs, key)
        for key in range(2, pairs, 2)
        if key != last
    }
    most = total([parts[0]] + list(arrived.values()), [])
    rest = swap(after(parts[last // 2], comp_ops, arrived[2]), "pair", pairs, last)
    shape = (2, norms, sites, rows, cols)
    early = renorm(normals, range(1, sec), basis_split, None, shape)
    new_normal = renorm(normals, range(1), basis_split, early, shape, True)
    shape = (2, comps, sites, rows, cols)
    arrived = [far, comp_ops, near, (most, rest)]
    early = renorm(arrived, range(2), basis_split, site_part, shape, awaited=[most])
    return new_normal, renorm(arrived, range(2, sec), basis_split, early, shape, True)


def solution(mesh):
    placed = (
        P(None, "pair", None, "sec"),
        P(None, "pair", None),
        P(None, "pair", None, None),
        P(None, None, None, "sec"),
    )
    return jax.shard_map(
        functools.partial(on_device, mesh.shape["pair"], mesh.shape["sec"]),
        mesh=mesh,
        in_specs=placed,
        out_specs=(P(None, "pair", None, None, "sec"), P(None, "pair", None, None, "sec")),
        check_vma=False,
    )
```

```python
import functools

import jax
import jax.numpy as jnp
from jax import lax
from jax.experimental import pallas as pl
from jax.experimental.pallas import tpu as pltpu
from jax.sharding import PartitionSpec as P

VMEM_BYTES = 24 * 1024 * 1024
WIDE = 256
TILE = (8, 128)
VMEM = pl.BlockSpec(memory_space=pltpu.VMEM)
ANY = pl.BlockSpec(memory_space=pl.ANY)
HBM = pl.BlockSpec(memory_space=pltpu.HBM)


def call(kernel, out_shape, in_specs, flops, scratch_shapes=(), moved=4 << 20):
    return pl.pallas_call(
        kernel,
        out_shape=out_shape,
        in_specs=in_specs,
        out_specs=jax.tree.map(lambda _: VMEM, out_shape),
        scratch_shapes=scratch_shapes,
        cost_estimate=pl.CostEstimate(flops=flops, bytes_accessed=moved, transcendentals=0),
        compiler_params=pltpu.CompilerParams(vmem_limit_bytes=VMEM_BYTES),
    )


def split(x):
    high = x.astype(jnp.bfloat16)
    return high, (x - high.astype(jnp.float32)).astype(jnp.bfloat16)


def order(sec):
    return (1, 2, 0, 3) if sec == 4 else tuple(range(sec))


def prepare_kernel(depth, basis_hbm, site_hbm, integrals_ref, *refs):
    split_ref, part_ref, row_ref = refs[:3]
    scratch = refs[3:]
    row_ref[...] = integrals_ref[...]
    basis_ref, site_ref, basis_sem, site_sem = scratch
    _, sites, old, cols = basis_ref.shape
    rows = part_ref.shape[3]
    me = lax.axis_index("sec")
    site_copy = pltpu.make_async_copy(site_hbm, site_ref, site_sem)
    site_copy.start()
    copies = [
        (part, site, pltpu.make_async_copy(
            basis_hbm.at[part, site], basis_ref.at[part, site], basis_sem.at[part, site]
        ))
        for part in range(2)
        for site in range(sites)
    ]
    for _, _, copy in copies:
        copy.start()
    for part, site, copy in copies:
        copy.wait()
        for step, far in enumerate(order(old // depth)):
            start = pl.multiple_of((me ^ far) * depth, depth)
            high, low = split(basis_ref[part, site, pl.ds(start, depth), :])
            for which, value in enumerate((high, low, high)):
                at = pl.ds(((step * 3 + which) * 2 + part) * depth, depth)
                split_ref[at, pl.ds(site * cols, cols)] = value
    site_copy.wait()
    for comp in range(part_ref.shape[1]):
        for site in range(sites):
            real = imag = None
            for other in range(sites):
                sr, si = site_ref[0, comp, site, other], site_ref[1, comp, site, other]
                br, bi = basis_ref[0, other, :rows, :], basis_ref[1, other, :rows, :]
                tr, ti = sr * br - si * bi, sr * bi + si * br
                real = tr if real is None else real + tr
                imag = ti if imag is None else imag + ti
            part_ref[0, comp, site] = real
            part_ref[1, comp, site] = imag


def prepare(basis, site_terms, integrals, rows, depth):
    _, sites, old, cols = basis.shape
    comps = site_terms.shape[1]
    halves = jax.ShapeDtypeStruct((6 * old, sites * cols), jnp.bfloat16)
    part = jax.ShapeDtypeStruct((2, comps, sites, rows, cols), jnp.float32)
    return call(
        functools.partial(prepare_kernel, depth),
        (halves, part, jax.ShapeDtypeStruct(integrals.shape, integrals.dtype)),
        [HBM, HBM, VMEM],
        8 * comps * sites * sites * rows * cols,
        [
            pltpu.VMEM(basis.shape, basis.dtype),
            pltpu.SMEM(site_terms.shape, site_terms.dtype),
            pltpu.SemaphoreType.DMA((2, sites)),
            pltpu.SemaphoreType.DMA,
        ],
        4 << 20,
    )(basis, site_terms, integrals)


def pack(block, tables):
    _, per, rows, cols = block.shape

    def kernel(block_ref, *refs):
        out_ref = refs[-1]
        out_ref[:, :, :rows, :] = block_ref[...]
        out_ref[:, :, rows:, :] = jnp.zeros((2, per) + TILE, jnp.float32)
        for under, ref in enumerate(refs[:-1]):
            _, comps, norms = ref.shape
            for part in range(2):
                first = rows + part * comps
                out_ref[under, 0, first : first + comps, :norms] = ref[part]

    out = jax.ShapeDtypeStruct((2, per, rows + TILE[0], cols), block.dtype)
    return call(kernel, out, [VMEM] * (1 + len(tables)), 0)(block, *tables)


def after(x, *others):
    def kernel(x_ref, *refs):
        refs[-1][...] = x_ref[...]

    out = jax.ShapeDtypeStruct(x.shape, x.dtype)
    return call(kernel, out, [VMEM] + [ANY] * len(others), 0)(x, *others)


def renorm_kernel(steps, parts, carried, awaited, streamed, *refs):
    count = sum(parts)
    split_ref = refs[count]
    first = count + 1 + carried + awaited
    out_ref, left = refs[first : first + 2]
    out_hbm, out_ref, sems = (out_ref,) + refs[-2:] if streamed else (None, out_ref, None)
    _, ops, sites, rows, cols = out_ref.shape
    depth = refs[0].shape[-1]
    tall = ops * rows
    for step in range(len(steps)):
        first = sum(parts[:step])
        value = sum(refs[at][:, :, :rows, :] for at in range(first + 1, first + parts[step]))
        value = (refs[first][:, :, :rows, :] + value).reshape(2, tall, depth)
        (rh, rl), (ih, il) = split(value[0]), split(value[1])
        for which, (real, imag) in enumerate(((rh, ih), (rh, ih), (rl, il))):
            at = 2 * (step * 3 + which) * depth
            left[:tall, at : at + depth] = real
            left[:tall, at + depth : at + 2 * depth] = -imag
            left[tall:, at : at + depth] = imag
            left[tall:, at + depth : at + 2 * depth] = real
    deep = slice(6 * depth * steps[0], 6 * depth * (steps[-1] + 1))
    copies = []
    for first in range(0, sites * cols, WIDE):
        at = (deep, slice(first, first + WIDE))
        total = jnp.dot(left[...], split_ref[at], preferred_element_type=jnp.float32)
        some = range(first // cols, (first + WIDE) // cols)
        for part in range(2):
            for op in range(ops):
                for site in some:
                    across = slice(site * cols - first, site * cols - first + cols)
                    start = part * tall + op * rows
                    value = total[start : start + rows, across]
                    if carried:
                        value = value + refs[count + 1][part, op, site]
                    out_ref[part, op, site] = value
                if streamed:
                    piece = (part, op, pl.ds(some.start, len(some)))
                    copies.append(
                        pltpu.make_async_copy(
                            out_ref.at[piece], out_hbm.at[piece], sems.at[len(copies)]
                        )
                    )
                    copies[-1].start()
    for copy in copies:
        copy.wait()


def renorm(blocks, steps, basis, carry, shape, streamed=False, awaited=()):
    blocks = [block if isinstance(block, tuple) else (block,) for block in blocks]
    blocks = blocks[steps.start : steps.stop]
    parts = tuple(len(block) for block in blocks)
    args = sum(blocks, ()) + (basis,) + (() if carry is None else (carry,))
    _, ops, sites, rows, cols = shape
    depth = blocks[0][0].shape[-1]
    left = pltpu.VMEM((2 * ops * rows, 6 * depth * len(blocks)), jnp.bfloat16)
    pieces = 2 * ops * sites * cols // WIDE
    held = [pltpu.VMEM(shape, jnp.float32), pltpu.SemaphoreType.DMA((pieces,))]
    return pl.pallas_call(
        functools.partial(
            renorm_kernel, steps, parts, carry is not None, len(awaited), streamed
        ),
        out_shape=jax.ShapeDtypeStruct(shape, jnp.float32),
        in_specs=[VMEM] * len(args) + [ANY] * len(awaited),
        out_specs=HBM if streamed else VMEM,
        scratch_shapes=[left] + (held if streamed else []),
        cost_estimate=pl.CostEstimate(
            flops=24 * ops * rows * depth * len(blocks) * sites * cols,
            bytes_accessed=4 << 20,
            transcendentals=0,
        ),
        compiler_params=pltpu.CompilerParams(vmem_limit_bytes=VMEM_BYTES),
    )(*args, *awaited)


def total(parts, awaited):
    def kernel(*refs):
        refs[-1][...] = sum((ref[...] for ref in refs[1 : len(parts)]), refs[0][...])

    out = jax.ShapeDtypeStruct(parts[0].shape, parts[0].dtype)
    specs = [VMEM] * len(parts) + [ANY] * len(awaited)
    return call(kernel, out, specs, out.size * len(parts))(*parts, *awaited)


def combine_kernel(operators, tables, per, *refs):
    outs = refs[len(refs) - len(tables) :]
    comps, rows, _ = outs[0].shape[1:]
    me = lax.axis_index("pair")
    for (held, under), out_ref in zip(tables, outs):
        lane = lax.broadcasted_iota(jnp.int32, (1, refs[held].shape[-1]), 1)
        for comp in range(comps):
            real = imag = None
            for array, place, op, key in operators:
                coefficients = []
                for part in range(2):
                    at = part * comps + comp
                    if under is None:
                        row = refs[held][part, comp : comp + 1, :]
                    else:
                        row = refs[held][under, 0, rows + at : rows + at + 1, :]
                    here = jnp.where(lane == (me ^ key) * per + op, row, 0.0)
                    coefficients.append(jnp.sum(here, axis=1, keepdims=True))
                cr, ci = coefficients
                br, bi = (refs[array][part, place, :rows, :] for part in range(2))
                tr, ti = cr * br - ci * bi, cr * bi + ci * br
                real = tr if real is None else real + tr
                imag = ti if imag is None else imag + ti
            out_ref[0, comp] = real
            out_ref[1, comp] = imag


def combine(arrays, operators, tables, per, shape, awaited=()):
    rows, cols = shape[2:]
    return call(
        functools.partial(combine_kernel, operators, tables, per),
        (jax.ShapeDtypeStruct(shape, jnp.float32),) * len(tables),
        [VMEM] * len(arrays) + [ANY] * len(awaited),
        8 * len(tables) * len(operators) * rows * cols,
        moved=4 << 20,
    )(*arrays, *awaited)


def swap(x, axis, size, key):
    return lax.ppermute(x, axis, [(at, at ^ key) for at in range(size)])


def chip_blocks(own, row, beside, pairs):
    per = own.shape[1]
    arrays, tables = [own], []
    operators = [(0, op, op, 0) for op in range(per)]
    if pairs == 8:
        for key in (2, 4):
            operators += [(len(arrays), op, op, key) for op in range(per)]
            arrays.append(swap(own, "pair", pairs, key))
        operators += [(3, op, op, 6) for op in range(per)]
        arrays += [
            swap(pack(arrays[1], [row, beside]), "pair", pairs, 4),
            row,
            beside,
        ]
        tables = [(4, None), (5, None), (3, 0), (3, 1)]
    else:
        arrays[0] = pack(own, [row])
        tables = [(0, 0)]
        for key in range(2, pairs, 2):
            operators += [(len(arrays), op, op, key) for op in range(per)]
            tables.append((len(arrays), 0))
            arrays.append(swap(arrays[0], "pair", pairs, key))
    return arrays, operators, tables


def on_device(pairs, sec, normal_ops, integrals, site_terms, basis):
    _, norms, rows, depth = normal_ops.shape
    _, sites, _, cols = basis.shape
    comps = integrals.shape[1]
    shape = (2, comps, rows, depth)
    two = swap(normal_ops, "sec", sec, 2)
    one = swap(normal_ops, "sec", sec, 1)
    beside = swap(integrals, "pair", pairs, 2)
    sibling = swap(integrals, "pair", pairs, 1)
    basis_split, site_part, row = prepare(basis, site_terms, integrals, rows, depth)
    arrays, operators, tables = chip_blocks(normal_ops, row, beside, pairs)
    two = after(two, sibling)
    three = swap(two, "sec", sec, 1)
    two = after(after(two, one), arrays[2])
    normals = [one, two, normal_ops, three]
    held = arrays + [row, sibling]
    here = [(len(arrays), None), (len(arrays) + 1, None)]
    mine, other = combine(held, operators, here, norms, shape)
    held = [two, swap(two, "pair", pairs, 1)] + arrays
    operators = [(key, op, op, key) for key in range(2) for op in range(norms)]
    tables = [(2 + at, part) for at, part in tables]
    parts = combine(held, operators, tables, norms, shape)
    comp_ops = total([mine, swap(other, "pair", pairs, 1)], [parts[0]])
    far = swap(comp_ops, "sec", sec, 3)
    near = swap(after(comp_ops, three), "sec", sec, 1)
    summed = [parts[0]] + [
        swap(after(part, comp_ops), "pair", pairs, key)
        for part, key in zip(parts[1:], range(2, pairs, 2))
    ]
    shape = (2, norms, sites, rows, cols)
    early = renorm(normals, range(sec - 1), basis_split, None, shape)
    new_normal = renorm(normals, range(sec - 1, sec), basis_split, early, shape, True)
    shape = (2, comps, sites, rows, cols)
    arrived = [near, tuple(summed), comp_ops, far]
    early = renorm(arrived, range(2, sec), basis_split, site_part, shape)
    early = renorm(arrived, range(1, 2), basis_split, early, shape)
    return new_normal, renorm(arrived, range(1), basis_split, early, shape, True)


def solution(mesh):
    placed = (
        P(None, "pair", None, "sec"),
        P(None, "pair", None),
        P(None, "pair", None, None),
        P(None, None, None, "sec"),
    )
    return jax.shard_map(
        functools.partial(on_device, mesh.shape["pair"], mesh.shape["sec"]),
        mesh=mesh,
        in_specs=placed,
        out_specs=(P(None, "pair", None, None, "sec"), P(None, "pair", None, None, "sec")),
        check_vma=False,
    )
```

```python
import functools

import jax
import jax.numpy as jnp
from jax import lax
from jax.experimental import pallas as pl
from jax.experimental.pallas import tpu as pltpu
from jax.sharding import PartitionSpec as P

VMEM_BYTES = 24 * 1024 * 1024
WIDE = 256
TILE = (8, 128)
VMEM = pl.BlockSpec(memory_space=pltpu.VMEM)
ANY = pl.BlockSpec(memory_space=pl.ANY)
HBM = pl.BlockSpec(memory_space=pltpu.HBM)


def call(kernel, out_shape, in_specs, flops, scratch_shapes=(), moved=4 << 20):
    return pl.pallas_call(
        kernel,
        out_shape=out_shape,
        in_specs=in_specs,
        out_specs=jax.tree.map(lambda _: VMEM, out_shape),
        scratch_shapes=scratch_shapes,
        cost_estimate=pl.CostEstimate(flops=flops, bytes_accessed=moved, transcendentals=0),
        compiler_params=pltpu.CompilerParams(vmem_limit_bytes=VMEM_BYTES),
    )


def split(x):
    high = x.astype(jnp.bfloat16)
    return high, (x - high.astype(jnp.float32)).astype(jnp.bfloat16)


def order(sec):
    return (3, 1, 2, 0) if sec == 4 else tuple(range(sec))


def prepare_kernel(depth, basis_hbm, site_hbm, integrals_ref, *refs):
    split_ref, part_ref, row_ref = refs[:3]
    scratch = refs[3:]
    row_ref[...] = integrals_ref[...]
    basis_ref, site_ref, basis_sem, site_sem = scratch
    _, sites, old, cols = basis_ref.shape
    rows = part_ref.shape[3]
    me = lax.axis_index("sec")
    site_copy = pltpu.make_async_copy(site_hbm, site_ref, site_sem)
    site_copy.start()
    copies = [
        (part, site, pltpu.make_async_copy(
            basis_hbm.at[part, site], basis_ref.at[part, site], basis_sem.at[part, site]
        ))
        for part in range(2)
        for site in range(sites)
    ]
    for _, _, copy in copies:
        copy.start()
    for part, site, copy in copies:
        copy.wait()
        for step, far in enumerate(order(old // depth)):
            start = pl.multiple_of((me ^ far) * depth, depth)
            high, low = split(basis_ref[part, site, pl.ds(start, depth), :])
            for which, value in enumerate((high, low, high)):
                at = pl.ds(((step * 3 + which) * 2 + part) * depth, depth)
                split_ref[at, pl.ds(site * cols, cols)] = value
    site_copy.wait()
    for comp in range(part_ref.shape[1]):
        for site in range(sites):
            real = imag = None
            for other in range(sites):
                sr, si = site_ref[0, comp, site, other], site_ref[1, comp, site, other]
                br, bi = basis_ref[0, other, :rows, :], basis_ref[1, other, :rows, :]
                tr, ti = sr * br - si * bi, sr * bi + si * br
                real = tr if real is None else real + tr
                imag = ti if imag is None else imag + ti
            part_ref[0, comp, site] = real
            part_ref[1, comp, site] = imag


def prepare(basis, site_terms, integrals, rows, depth):
    _, sites, old, cols = basis.shape
    comps = site_terms.shape[1]
    halves = jax.ShapeDtypeStruct((6 * old, sites * cols), jnp.bfloat16)
    part = jax.ShapeDtypeStruct((2, comps, sites, rows, cols), jnp.float32)
    return call(
        functools.partial(prepare_kernel, depth),
        (halves, part, jax.ShapeDtypeStruct(integrals.shape, integrals.dtype)),
        [HBM, HBM, VMEM],
        8 * comps * sites * sites * rows * cols,
        [
            pltpu.VMEM(basis.shape, basis.dtype),
            pltpu.SMEM(site_terms.shape, site_terms.dtype),
            pltpu.SemaphoreType.DMA((2, sites)),
            pltpu.SemaphoreType.DMA,
        ],
        4 << 20,
    )(basis, site_terms, integrals)


def pack(block, tables):
    _, per, rows, cols = block.shape

    def kernel(block_ref, *refs):
        out_ref = refs[-1]
        out_ref[:, :, :rows, :] = block_ref[...]
        out_ref[:, :, rows:, :] = jnp.zeros((2, per) + TILE, jnp.float32)
        for under, ref in enumerate(refs[:-1]):
            _, comps, norms = ref.shape
            for part in range(2):
                first = rows + part * comps
                out_ref[under, 0, first : first + comps, :norms] = ref[part]

    out = jax.ShapeDtypeStruct((2, per, rows + TILE[0], cols), block.dtype)
    return call(kernel, out, [VMEM] * (1 + len(tables)), 0)(block, *tables)


def after(x, *others):
    def kernel(x_ref, *refs):
        refs[-1][...] = x_ref[...]

    out = jax.ShapeDtypeStruct(x.shape, x.dtype)
    return call(kernel, out, [VMEM] + [ANY] * len(others), 0)(x, *others)


def renorm_kernel(steps, parts, carried, awaited, streamed, *refs):
    count = sum(parts)
    split_ref = refs[count]
    first = count + 1 + carried + awaited
    out_ref, left = refs[first : first + 2]
    out_hbm, out_ref, sems = (out_ref,) + refs[-2:] if streamed else (None, out_ref, None)
    _, ops, sites, rows, cols = out_ref.shape
    depth = refs[0].shape[-1]
    tall = ops * rows
    for step in range(len(steps)):
        first = sum(parts[:step])
        value = sum(refs[at][:, :, :rows, :] for at in range(first + 1, first + parts[step]))
        value = (refs[first][:, :, :rows, :] + value).reshape(2, tall, depth)
        (rh, rl), (ih, il) = split(value[0]), split(value[1])
        for which, (real, imag) in enumerate(((rh, ih), (rh, ih), (rl, il))):
            at = 2 * (step * 3 + which) * depth
            left[:tall, at : at + depth] = real
            left[:tall, at + depth : at + 2 * depth] = -imag
            left[tall:, at : at + depth] = imag
            left[tall:, at + depth : at + 2 * depth] = real
    deep = slice(6 * depth * steps[0], 6 * depth * (steps[-1] + 1))
    copies = []
    for first in range(0, sites * cols, WIDE):
        at = (deep, slice(first, first + WIDE))
        total = jnp.dot(left[...], split_ref[at], preferred_element_type=jnp.float32)
        some = range(first // cols, (first + WIDE) // cols)
        for part in range(2):
            for op in range(ops):
                for site in some:
                    across = slice(site * cols - first, site * cols - first + cols)
                    start = part * tall + op * rows
                    value = total[start : start + rows, across]
                    if carried:
                        value = value + refs[count + 1][part, op, site]
                    out_ref[part, op, site] = value
                if streamed:
                    piece = (part, op, pl.ds(some.start, len(some)))
                    copies.append(
                        pltpu.make_async_copy(
                            out_ref.at[piece], out_hbm.at[piece], sems.at[len(copies)]
                        )
                    )
                    copies[-1].start()
    for copy in copies:
        copy.wait()


def renorm(blocks, steps, basis, carry, shape, streamed=False, awaited=()):
    blocks = [block if isinstance(block, tuple) else (block,) for block in blocks]
    blocks = blocks[steps.start : steps.stop]
    parts = tuple(len(block) for block in blocks)
    args = sum(blocks, ()) + (basis,) + (() if carry is None else (carry,))
    _, ops, sites, rows, cols = shape
    depth = blocks[0][0].shape[-1]
    left = pltpu.VMEM((2 * ops * rows, 6 * depth * len(blocks)), jnp.bfloat16)
    pieces = 2 * ops * sites * cols // WIDE
    held = [pltpu.VMEM(shape, jnp.float32), pltpu.SemaphoreType.DMA((pieces,))]
    return pl.pallas_call(
        functools.partial(
            renorm_kernel, steps, parts, carry is not None, len(awaited), streamed
        ),
        out_shape=jax.ShapeDtypeStruct(shape, jnp.float32),
        in_specs=[VMEM] * len(args) + [ANY] * len(awaited),
        out_specs=HBM if streamed else VMEM,
        scratch_shapes=[left] + (held if streamed else []),
        cost_estimate=pl.CostEstimate(
            flops=24 * ops * rows * depth * len(blocks) * sites * cols,
            bytes_accessed=4 << 20,
            transcendentals=0,
        ),
        compiler_params=pltpu.CompilerParams(vmem_limit_bytes=VMEM_BYTES),
    )(*args, *awaited)


def total(parts, awaited):
    def kernel(*refs):
        refs[-1][...] = sum((ref[...] for ref in refs[1 : len(parts)]), refs[0][...])

    out = jax.ShapeDtypeStruct(parts[0].shape, parts[0].dtype)
    specs = [VMEM] * len(parts) + [ANY] * len(awaited)
    return call(kernel, out, specs, out.size * len(parts))(*parts, *awaited)


def combine_kernel(operators, tables, per, *refs):
    outs = refs[len(refs) - len(tables) :]
    comps, rows, _ = outs[0].shape[1:]
    me = lax.axis_index("pair")
    for (held, under), out_ref in zip(tables, outs):
        lane = lax.broadcasted_iota(jnp.int32, (1, refs[held].shape[-1]), 1)
        for comp in range(comps):
            real = imag = None
            for array, place, op, key in operators:
                coefficients = []
                for part in range(2):
                    at = part * comps + comp
                    if under is None:
                        row = refs[held][part, comp : comp + 1, :]
                    else:
                        row = refs[held][under, 0, rows + at : rows + at + 1, :]
                    here = jnp.where(lane == (me ^ key) * per + op, row, 0.0)
                    coefficients.append(jnp.sum(here, axis=1, keepdims=True))
                cr, ci = coefficients
                br, bi = (refs[array][part, place, :rows, :] for part in range(2))
                tr, ti = cr * br - ci * bi, cr * bi + ci * br
                real = tr if real is None else real + tr
                imag = ti if imag is None else imag + ti
            out_ref[0, comp] = real
            out_ref[1, comp] = imag


def combine(arrays, operators, tables, per, shape, awaited=()):
    rows, cols = shape[2:]
    return call(
        functools.partial(combine_kernel, operators, tables, per),
        (jax.ShapeDtypeStruct(shape, jnp.float32),) * len(tables),
        [VMEM] * len(arrays) + [ANY] * len(awaited),
        8 * len(tables) * len(operators) * rows * cols,
        moved=4 << 20,
    )(*arrays, *awaited)


def swap(x, axis, size, key):
    return lax.ppermute(x, axis, [(at, at ^ key) for at in range(size)])


def chip_blocks(own, row, beside, pairs):
    per = own.shape[1]
    arrays, tables = [own], []
    operators = [(0, op, op, 0) for op in range(per)]
    if pairs == 8:
        for key in (2, 4):
            operators += [(len(arrays), op, op, key) for op in range(per)]
            arrays.append(swap(own, "pair", pairs, key))
        operators += [(3, op, op, 6) for op in range(per)]
        arrays += [
            swap(pack(arrays[1], [row, beside]), "pair", pairs, 4),
            row,
            beside,
        ]
        tables = [(4, None), (5, None), (3, 0), (3, 1)]
    else:
        arrays[0] = pack(own, [row])
        tables = [(0, 0)]
        for key in range(2, pairs, 2):
            operators += [(len(arrays), op, op, key) for op in range(per)]
            tables.append((len(arrays), 0))
            arrays.append(swap(arrays[0], "pair", pairs, key))
    return arrays, operators, tables


def on_device(pairs, sec, normal_ops, integrals, site_terms, basis):
    _, norms, rows, depth = normal_ops.shape
    _, sites, _, cols = basis.shape
    comps = integrals.shape[1]
    shape = (2, comps, rows, depth)
    two = swap(normal_ops, "sec", sec, 2)
    one = swap(normal_ops, "sec", sec, 1)
    beside = swap(integrals, "pair", pairs, 2)
    sibling = swap(integrals, "pair", pairs, 1)
    basis_split, site_part, row = prepare(basis, site_terms, integrals, rows, depth)
    arrays, operators, tables = chip_blocks(normal_ops, row, beside, pairs)
    two = after(two, sibling)
    three = swap(two, "sec", sec, 1)
    two = after(after(two, one), arrays[2])
    normals = [three, one, two, normal_ops]
    held = arrays + [row, sibling]
    here = [(len(arrays), None), (len(arrays) + 1, None)]
    mine, other = combine(held, operators, here, norms, shape)
    held = [two, swap(two, "pair", pairs, 1)] + arrays
    operators = [(key, op, op, key) for key in range(2) for op in range(norms)]
    tables = [(2 + at, part) for at, part in tables]
    parts = combine(held, operators, tables, norms, shape)
    comp_ops = total([mine, swap(other, "pair", pairs, 1)], [parts[0]])
    far = swap(comp_ops, "sec", sec, 3)
    near = swap(comp_ops, "sec", sec, 1)
    summed = [parts[0]]
    for key in range(2, pairs, 2):
        part = after(parts[key // 2], comp_ops)
        if key == 2:
            part = after(part, three)
        summed.append(swap(part, "pair", pairs, key))
    shape = (2, norms, sites, rows, cols)
    early = renorm(normals, range(1, sec), basis_split, None, shape)
    new_normal = renorm(normals, range(1), basis_split, early, shape, True)
    shape = (2, comps, sites, rows, cols)
    arrived = [far, near, tuple(summed), comp_ops]
    early = renorm(arrived, range(3, sec), basis_split, site_part, shape)
    return new_normal, renorm(arrived, range(3), basis_split, early, shape, True)


def solution(mesh):
    placed = (
        P(None, "pair", None, "sec"),
        P(None, "pair", None),
        P(None, "pair", None, None),
        P(None, None, None, "sec"),
    )
    return jax.shard_map(
        functools.partial(on_device, mesh.shape["pair"], mesh.shape["sec"]),
        mesh=mesh,
        in_specs=placed,
        out_specs=(P(None, "pair", None, None, "sec"), P(None, "pair", None, None, "sec")),
        check_vma=False,
    )
```

```python
import functools

import jax
import jax.numpy as jnp
from jax import lax
from jax.experimental import pallas as pl
from jax.experimental.pallas import tpu as pltpu
from jax.sharding import PartitionSpec as P

VMEM_BYTES = 24 * 1024 * 1024
WIDE = 256
TILE = (8, 128)
VMEM = pl.BlockSpec(memory_space=pltpu.VMEM)
ANY = pl.BlockSpec(memory_space=pl.ANY)
HBM = pl.BlockSpec(memory_space=pltpu.HBM)


def call(kernel, out_shape, in_specs, flops, scratch_shapes=(), moved=4 << 20):
    return pl.pallas_call(
        kernel,
        out_shape=out_shape,
        in_specs=in_specs,
        out_specs=jax.tree.map(lambda _: VMEM, out_shape),
        scratch_shapes=scratch_shapes,
        cost_estimate=pl.CostEstimate(flops=flops, bytes_accessed=moved, transcendentals=0),
        compiler_params=pltpu.CompilerParams(vmem_limit_bytes=VMEM_BYTES),
    )


def split(x):
    high = x.astype(jnp.bfloat16)
    return high, (x - high.astype(jnp.float32)).astype(jnp.bfloat16)


def order(sec):
    return (3, 1, 2, 0) if sec == 4 else tuple(range(sec))


def prepare_kernel(depth, basis_hbm, site_hbm, integrals_ref, *refs):
    split_ref, part_ref, row_ref = refs[:3]
    scratch = refs[3:]
    row_ref[...] = integrals_ref[...]
    basis_ref, site_ref, basis_sem, site_sem = scratch
    _, sites, old, cols = basis_ref.shape
    rows = part_ref.shape[3]
    me = lax.axis_index("sec")
    site_copy = pltpu.make_async_copy(site_hbm, site_ref, site_sem)
    site_copy.start()
    copies = [
        (part, site, pltpu.make_async_copy(
            basis_hbm.at[part, site], basis_ref.at[part, site], basis_sem.at[part, site]
        ))
        for part in range(2)
        for site in range(sites)
    ]
    for _, _, copy in copies:
        copy.start()
    for part, site, copy in copies:
        copy.wait()
        for step, far in enumerate(order(old // depth)):
            start = pl.multiple_of((me ^ far) * depth, depth)
            high, low = split(basis_ref[part, site, pl.ds(start, depth), :])
            for which, value in enumerate((high, low, high)):
                at = pl.ds(((step * 3 + which) * 2 + part) * depth, depth)
                split_ref[at, pl.ds(site * cols, cols)] = value
    site_copy.wait()
    for comp in range(part_ref.shape[1]):
        for site in range(sites):
            real = imag = None
            for other in range(sites):
                sr, si = site_ref[0, comp, site, other], site_ref[1, comp, site, other]
                br, bi = basis_ref[0, other, :rows, :], basis_ref[1, other, :rows, :]
                tr, ti = sr * br - si * bi, sr * bi + si * br
                real = tr if real is None else real + tr
                imag = ti if imag is None else imag + ti
            part_ref[0, comp, site] = real
            part_ref[1, comp, site] = imag


def prepare(basis, site_terms, integrals, rows, depth):
    _, sites, old, cols = basis.shape
    comps = site_terms.shape[1]
    halves = jax.ShapeDtypeStruct((6 * old, sites * cols), jnp.bfloat16)
    part = jax.ShapeDtypeStruct((2, comps, sites, rows, cols), jnp.float32)
    return call(
        functools.partial(prepare_kernel, depth),
        (halves, part, jax.ShapeDtypeStruct(integrals.shape, integrals.dtype)),
        [HBM, HBM, VMEM],
        8 * comps * sites * sites * rows * cols,
        [
            pltpu.VMEM(basis.shape, basis.dtype),
            pltpu.SMEM(site_terms.shape, site_terms.dtype),
            pltpu.SemaphoreType.DMA((2, sites)),
            pltpu.SemaphoreType.DMA,
        ],
        4 << 20,
    )(basis, site_terms, integrals)


def pack(block, tables):
    _, per, rows, cols = block.shape

    def kernel(block_ref, *refs):
        out_ref = refs[-1]
        out_ref[:, :, :rows, :] = block_ref[...]
        out_ref[:, :, rows:, :] = jnp.zeros((2, per) + TILE, jnp.float32)
        for under, ref in enumerate(refs[:-1]):
            _, comps, norms = ref.shape
            for part in range(2):
                first = rows + part * comps
                out_ref[under, 0, first : first + comps, :norms] = ref[part]

    out = jax.ShapeDtypeStruct((2, per, rows + TILE[0], cols), block.dtype)
    return call(kernel, out, [VMEM] * (1 + len(tables)), 0)(block, *tables)


def after(x, *others):
    def kernel(x_ref, *refs):
        refs[-1][...] = x_ref[...]

    out = jax.ShapeDtypeStruct(x.shape, x.dtype)
    return call(kernel, out, [VMEM] + [ANY] * len(others), 0)(x, *others)


def renorm_kernel(steps, parts, carried, awaited, streamed, *refs):
    count = sum(parts)
    split_ref = refs[count]
    first = count + 1 + carried + awaited
    out_ref, left = refs[first : first + 2]
    out_hbm, out_ref, sems = (out_ref,) + refs[-2:] if streamed else (None, out_ref, None)
    _, ops, sites, rows, cols = out_ref.shape
    depth = refs[0].shape[-1]
    tall = ops * rows
    for step in range(len(steps)):
        first = sum(parts[:step])
        value = sum(refs[at][:, :, :rows, :] for at in range(first + 1, first + parts[step]))
        value = (refs[first][:, :, :rows, :] + value).reshape(2, tall, depth)
        (rh, rl), (ih, il) = split(value[0]), split(value[1])
        for which, (real, imag) in enumerate(((rh, ih), (rh, ih), (rl, il))):
            at = 2 * (step * 3 + which) * depth
            left[:tall, at : at + depth] = real
            left[:tall, at + depth : at + 2 * depth] = -imag
            left[tall:, at : at + depth] = imag
            left[tall:, at + depth : at + 2 * depth] = real
    deep = slice(6 * depth * steps[0], 6 * depth * (steps[-1] + 1))
    copies = []
    for first in range(0, sites * cols, WIDE):
        at = (deep, slice(first, first + WIDE))
        total = jnp.dot(left[...], split_ref[at], preferred_element_type=jnp.float32)
        some = range(first // cols, (first + WIDE) // cols)
        for part in range(2):
            for op in range(ops):
                for site in some:
                    across = slice(site * cols - first, site * cols - first + cols)
                    start = part * tall + op * rows
                    value = total[start : start + rows, across]
                    if carried:
                        value = value + refs[count + 1][part, op, site]
                    out_ref[part, op, site] = value
                if streamed:
                    piece = (part, op, pl.ds(some.start, len(some)))
                    copies.append(
                        pltpu.make_async_copy(
                            out_ref.at[piece], out_hbm.at[piece], sems.at[len(copies)]
                        )
                    )
                    copies[-1].start()
    for copy in copies:
        copy.wait()


def renorm(blocks, steps, basis, carry, shape, streamed=False, awaited=()):
    blocks = [block if isinstance(block, tuple) else (block,) for block in blocks]
    blocks = blocks[steps.start : steps.stop]
    parts = tuple(len(block) for block in blocks)
    args = sum(blocks, ()) + (basis,) + (() if carry is None else (carry,))
    _, ops, sites, rows, cols = shape
    depth = blocks[0][0].shape[-1]
    left = pltpu.VMEM((2 * ops * rows, 6 * depth * len(blocks)), jnp.bfloat16)
    pieces = 2 * ops * sites * cols // WIDE
    held = [pltpu.VMEM(shape, jnp.float32), pltpu.SemaphoreType.DMA((pieces,))]
    return pl.pallas_call(
        functools.partial(
            renorm_kernel, steps, parts, carry is not None, len(awaited), streamed
        ),
        out_shape=jax.ShapeDtypeStruct(shape, jnp.float32),
        in_specs=[VMEM] * len(args) + [ANY] * len(awaited),
        out_specs=HBM if streamed else VMEM,
        scratch_shapes=[left] + (held if streamed else []),
        cost_estimate=pl.CostEstimate(
            flops=24 * ops * rows * depth * len(blocks) * sites * cols,
            bytes_accessed=4 << 20,
            transcendentals=0,
        ),
        compiler_params=pltpu.CompilerParams(vmem_limit_bytes=VMEM_BYTES),
    )(*args, *awaited)


def total(parts, awaited):
    def kernel(*refs):
        refs[-1][...] = sum((ref[...] for ref in refs[1 : len(parts)]), refs[0][...])

    out = jax.ShapeDtypeStruct(parts[0].shape, parts[0].dtype)
    specs = [VMEM] * len(parts) + [ANY] * len(awaited)
    return call(kernel, out, specs, out.size * len(parts))(*parts, *awaited)


def combine_kernel(operators, tables, per, *refs):
    outs = refs[len(refs) - len(tables) :]
    comps, rows, _ = outs[0].shape[1:]
    me = lax.axis_index("pair")
    for (held, under), out_ref in zip(tables, outs):
        lane = lax.broadcasted_iota(jnp.int32, (1, refs[held].shape[-1]), 1)
        for comp in range(comps):
            real = imag = None
            for array, place, op, key in operators:
                coefficients = []
                for part in range(2):
                    at = part * comps + comp
                    if under is None:
                        row = refs[held][part, comp : comp + 1, :]
                    else:
                        row = refs[held][under, 0, rows + at : rows + at + 1, :]
                    here = jnp.where(lane == (me ^ key) * per + op, row, 0.0)
                    coefficients.append(jnp.sum(here, axis=1, keepdims=True))
                cr, ci = coefficients
                br, bi = (refs[array][part, place, :rows, :] for part in range(2))
                tr, ti = cr * br - ci * bi, cr * bi + ci * br
                real = tr if real is None else real + tr
                imag = ti if imag is None else imag + ti
            out_ref[0, comp] = real
            out_ref[1, comp] = imag


def combine(arrays, operators, tables, per, shape, awaited=()):
    rows, cols = shape[2:]
    return call(
        functools.partial(combine_kernel, operators, tables, per),
        (jax.ShapeDtypeStruct(shape, jnp.float32),) * len(tables),
        [VMEM] * len(arrays) + [ANY] * len(awaited),
        8 * len(tables) * len(operators) * rows * cols,
        moved=4 << 20,
    )(*arrays, *awaited)


def swap(x, axis, size, key):
    return lax.ppermute(x, axis, [(at, at ^ key) for at in range(size)])


def chip_blocks(own, row, beside, pairs):
    per = own.shape[1]
    arrays, tables = [own], []
    operators = [(0, op, op, 0) for op in range(per)]
    if pairs == 8:
        for key in (2, 4):
            operators += [(len(arrays), op, op, key) for op in range(per)]
            arrays.append(swap(own, "pair", pairs, key))
        operators += [(3, op, op, 6) for op in range(per)]
        arrays += [
            swap(pack(arrays[1], [row, beside]), "pair", pairs, 4),
            row,
            beside,
        ]
        tables = [(4, None), (5, None), (3, 0), (3, 1)]
    else:
        arrays[0] = pack(own, [row])
        tables = [(0, 0)]
        for key in range(2, pairs, 2):
            operators += [(len(arrays), op, op, key) for op in range(per)]
            tables.append((len(arrays), 0))
            arrays.append(swap(arrays[0], "pair", pairs, key))
    return arrays, operators, tables


def on_device(pairs, sec, normal_ops, integrals, site_terms, basis):
    _, norms, rows, depth = normal_ops.shape
    _, sites, _, cols = basis.shape
    comps = integrals.shape[1]
    shape = (2, comps, rows, depth)
    two = swap(normal_ops, "sec", sec, 2)
    one = swap(normal_ops, "sec", sec, 1)
    beside = swap(integrals, "pair", pairs, 2)
    sibling = swap(integrals, "pair", pairs, 1)
    basis_split, site_part, row = prepare(basis, site_terms, integrals, rows, depth)
    arrays, operators, tables = chip_blocks(normal_ops, row, beside, pairs)
    two = after(two, sibling)
    three = swap(two, "sec", sec, 1)
    two = after(after(two, one), arrays[2])
    normals = [three, one, two, normal_ops]
    held = arrays + [row, sibling]
    here = [(len(arrays), None), (len(arrays) + 1, None)]
    mine, other = combine(held, operators, here, norms, shape)
    held = [two, swap(two, "pair", pairs, 1)] + arrays
    operators = [(key, op, op, key) for key in range(2) for op in range(norms)]
    tables = [(2 + at, part) for at, part in tables]
    parts = combine(held, operators, tables, norms, shape)
    comp_ops = total([mine, swap(other, "pair", pairs, 1)], [parts[0]])
    far = swap(comp_ops, "sec", sec, 3)
    near = swap(comp_ops, "sec", sec, 1)
    first = swap(parts[-1], "pair", pairs, pairs - 2)
    summed = [parts[0], first]
    for key in range(2, pairs - 2, 2):
        part = after(parts[key // 2], comp_ops)
        if key == 2:
            part = after(part, first)
        summed.append(swap(part, "pair", pairs, key))
    shape = (2, norms, sites, rows, cols)
    early = renorm(normals, range(1, sec), basis_split, None, shape)
    new_normal = renorm(normals, range(1), basis_split, early, shape, True)
    shape = (2, comps, sites, rows, cols)
    arrived = [far, near, tuple(summed), comp_ops]
    early = renorm(arrived, range(3, sec), basis_split, site_part, shape)
    return new_normal, renorm(arrived, range(3), basis_split, early, shape, True)


def solution(mesh):
    placed = (
        P(None, "pair", None, "sec"),
        P(None, "pair", None),
        P(None, "pair", None, None),
        P(None, None, None, "sec"),
    )
    return jax.shard_map(
        functools.partial(on_device, mesh.shape["pair"], mesh.shape["sec"]),
        mesh=mesh,
        in_specs=placed,
        out_specs=(P(None, "pair", None, None, "sec"), P(None, "pair", None, None, "sec")),
        check_vma=False,
    )
```

```python
import functools

import jax
import jax.numpy as jnp
from jax import lax
from jax.experimental import pallas as pl
from jax.experimental.pallas import tpu as pltpu
from jax.sharding import PartitionSpec as P

VMEM_BYTES = 24 * 1024 * 1024
WIDE = 256
TILE = (8, 128)
VMEM = pl.BlockSpec(memory_space=pltpu.VMEM)
ANY = pl.BlockSpec(memory_space=pl.ANY)
HBM = pl.BlockSpec(memory_space=pltpu.HBM)


def call(kernel, out_shape, in_specs, flops, scratch_shapes=(), moved=4 << 20):
    return pl.pallas_call(
        kernel,
        out_shape=out_shape,
        in_specs=in_specs,
        out_specs=jax.tree.map(lambda _: VMEM, out_shape),
        scratch_shapes=scratch_shapes,
        cost_estimate=pl.CostEstimate(flops=flops, bytes_accessed=moved, transcendentals=0),
        compiler_params=pltpu.CompilerParams(vmem_limit_bytes=VMEM_BYTES),
    )


def split(x):
    high = x.astype(jnp.bfloat16)
    return high, (x - high.astype(jnp.float32)).astype(jnp.bfloat16)


def order(sec):
    return (3, 1, 2, 0) if sec == 4 else tuple(range(sec))


def prepare_kernel(depth, basis_hbm, site_hbm, integrals_ref, *refs):
    split_ref, part_ref, row_ref = refs[:3]
    scratch = refs[3:]
    row_ref[...] = integrals_ref[...]
    basis_ref, site_ref, basis_sem, site_sem = scratch
    _, sites, old, cols = basis_ref.shape
    rows = part_ref.shape[3]
    me = lax.axis_index("sec")
    site_copy = pltpu.make_async_copy(site_hbm, site_ref, site_sem)
    site_copy.start()
    copies = [
        (part, site, pltpu.make_async_copy(
            basis_hbm.at[part, site], basis_ref.at[part, site], basis_sem.at[part, site]
        ))
        for part in range(2)
        for site in range(sites)
    ]
    for _, _, copy in copies:
        copy.start()
    for part, site, copy in copies:
        copy.wait()
        for step, far in enumerate(order(old // depth)):
            start = pl.multiple_of((me ^ far) * depth, depth)
            high, low = split(basis_ref[part, site, pl.ds(start, depth), :])
            for which, value in enumerate((high, low, high)):
                at = pl.ds(((step * 3 + which) * 2 + part) * depth, depth)
                split_ref[at, pl.ds(site * cols, cols)] = value
    site_copy.wait()
    for comp in range(part_ref.shape[1]):
        for site in range(sites):
            real = imag = None
            for other in range(sites):
                sr, si = site_ref[0, comp, site, other], site_ref[1, comp, site, other]
                br, bi = basis_ref[0, other, :rows, :], basis_ref[1, other, :rows, :]
                tr, ti = sr * br - si * bi, sr * bi + si * br
                real = tr if real is None else real + tr
                imag = ti if imag is None else imag + ti
            part_ref[0, comp, site] = real
            part_ref[1, comp, site] = imag


def prepare(basis, site_terms, integrals, rows, depth):
    _, sites, old, cols = basis.shape
    comps = site_terms.shape[1]
    halves = jax.ShapeDtypeStruct((6 * old, sites * cols), jnp.bfloat16)
    part = jax.ShapeDtypeStruct((2, comps, sites, rows, cols), jnp.float32)
    return call(
        functools.partial(prepare_kernel, depth),
        (halves, part, jax.ShapeDtypeStruct(integrals.shape, integrals.dtype)),
        [HBM, HBM, VMEM],
        8 * comps * sites * sites * rows * cols,
        [
            pltpu.VMEM(basis.shape, basis.dtype),
            pltpu.SMEM(site_terms.shape, site_terms.dtype),
            pltpu.SemaphoreType.DMA((2, sites)),
            pltpu.SemaphoreType.DMA,
        ],
        4 << 20,
    )(basis, site_terms, integrals)


def pack(block, tables):
    _, per, rows, cols = block.shape

    def kernel(block_ref, *refs):
        out_ref = refs[-1]
        out_ref[:, :, :rows, :] = block_ref[...]
        out_ref[:, :, rows:, :] = jnp.zeros((2, per) + TILE, jnp.float32)
        for under, ref in enumerate(refs[:-1]):
            _, comps, norms = ref.shape
            for part in range(2):
                first = rows + part * comps
                out_ref[under, 0, first : first + comps, :norms] = ref[part]

    out = jax.ShapeDtypeStruct((2, per, rows + TILE[0], cols), block.dtype)
    return call(kernel, out, [VMEM] * (1 + len(tables)), 0)(block, *tables)


def after(x, *others):
    def kernel(x_ref, *refs):
        refs[-1][...] = x_ref[...]

    out = jax.ShapeDtypeStruct(x.shape, x.dtype)
    return call(kernel, out, [VMEM] + [ANY] * len(others), 0)(x, *others)


def renorm_kernel(steps, parts, carried, awaited, streamed, *refs):
    count = sum(parts)
    split_ref = refs[count]
    first = count + 1 + carried + awaited
    out_ref, left = refs[first : first + 2]
    out_hbm, out_ref, sems = (out_ref,) + refs[-2:] if streamed else (None, out_ref, None)
    _, ops, sites, rows, cols = out_ref.shape
    depth = refs[0].shape[-1]
    tall = ops * rows
    for step in range(len(steps)):
        first = sum(parts[:step])
        value = sum(refs[at][:, :, :rows, :] for at in range(first + 1, first + parts[step]))
        value = (refs[first][:, :, :rows, :] + value).reshape(2, tall, depth)
        (rh, rl), (ih, il) = split(value[0]), split(value[1])
        for which, (real, imag) in enumerate(((rh, ih), (rh, ih), (rl, il))):
            at = 2 * (step * 3 + which) * depth
            left[:tall, at : at + depth] = real
            left[:tall, at + depth : at + 2 * depth] = -imag
            left[tall:, at : at + depth] = imag
            left[tall:, at + depth : at + 2 * depth] = real
    deep = slice(6 * depth * steps[0], 6 * depth * (steps[-1] + 1))
    copies = []
    for first in range(0, sites * cols, WIDE):
        at = (deep, slice(first, first + WIDE))
        total = jnp.dot(left[...], split_ref[at], preferred_element_type=jnp.float32)
        some = range(first // cols, (first + WIDE) // cols)
        for part in range(2):
            for op in range(ops):
                for site in some:
                    across = slice(site * cols - first, site * cols - first + cols)
                    start = part * tall + op * rows
                    value = total[start : start + rows, across]
                    if carried:
                        value = value + refs[count + 1][part, op, site]
                    out_ref[part, op, site] = value
                if streamed:
                    piece = (part, op, pl.ds(some.start, len(some)))
                    copies.append(
                        pltpu.make_async_copy(
                            out_ref.at[piece], out_hbm.at[piece], sems.at[len(copies)]
                        )
                    )
                    copies[-1].start()
    for copy in copies:
        copy.wait()


def renorm(blocks, steps, basis, carry, shape, streamed=False, awaited=()):
    blocks = [block if isinstance(block, tuple) else (block,) for block in blocks]
    blocks = blocks[steps.start : steps.stop]
    parts = tuple(len(block) for block in blocks)
    args = sum(blocks, ()) + (basis,) + (() if carry is None else (carry,))
    _, ops, sites, rows, cols = shape
    depth = blocks[0][0].shape[-1]
    left = pltpu.VMEM((2 * ops * rows, 6 * depth * len(blocks)), jnp.bfloat16)
    pieces = 2 * ops * sites * cols // WIDE
    held = [pltpu.VMEM(shape, jnp.float32), pltpu.SemaphoreType.DMA((pieces,))]
    return pl.pallas_call(
        functools.partial(
            renorm_kernel, steps, parts, carry is not None, len(awaited), streamed
        ),
        out_shape=jax.ShapeDtypeStruct(shape, jnp.float32),
        in_specs=[VMEM] * len(args) + [ANY] * len(awaited),
        out_specs=HBM if streamed else VMEM,
        scratch_shapes=[left] + (held if streamed else []),
        cost_estimate=pl.CostEstimate(
            flops=24 * ops * rows * depth * len(blocks) * sites * cols,
            bytes_accessed=4 << 20,
            transcendentals=0,
        ),
        compiler_params=pltpu.CompilerParams(vmem_limit_bytes=VMEM_BYTES),
    )(*args, *awaited)


def total(parts, awaited):
    def kernel(*refs):
        refs[-1][...] = sum((ref[...] for ref in refs[1 : len(parts)]), refs[0][...])

    out = jax.ShapeDtypeStruct(parts[0].shape, parts[0].dtype)
    specs = [VMEM] * len(parts) + [ANY] * len(awaited)
    return call(kernel, out, specs, out.size * len(parts))(*parts, *awaited)


def combine_kernel(operators, tables, per, *refs):
    outs = refs[len(refs) - len(tables) :]
    comps, rows, _ = outs[0].shape[1:]
    me = lax.axis_index("pair")
    for (held, under), out_ref in zip(tables, outs):
        lane = lax.broadcasted_iota(jnp.int32, (1, refs[held].shape[-1]), 1)
        for comp in range(comps):
            real = imag = None
            for array, place, op, key in operators:
                coefficients = []
                for part in range(2):
                    at = part * comps + comp
                    if under is None:
                        row = refs[held][part, comp : comp + 1, :]
                    else:
                        row = refs[held][under, 0, rows + at : rows + at + 1, :]
                    here = jnp.where(lane == (me ^ key) * per + op, row, 0.0)
                    coefficients.append(jnp.sum(here, axis=1, keepdims=True))
                cr, ci = coefficients
                br, bi = (refs[array][part, place, :rows, :] for part in range(2))
                tr, ti = cr * br - ci * bi, cr * bi + ci * br
                real = tr if real is None else real + tr
                imag = ti if imag is None else imag + ti
            out_ref[0, comp] = real
            out_ref[1, comp] = imag


def combine(arrays, operators, tables, per, shape, awaited=()):
    rows, cols = shape[2:]
    return call(
        functools.partial(combine_kernel, operators, tables, per),
        (jax.ShapeDtypeStruct(shape, jnp.float32),) * len(tables),
        [VMEM] * len(arrays) + [ANY] * len(awaited),
        8 * len(tables) * len(operators) * rows * cols,
        moved=4 << 20,
    )(*arrays, *awaited)


def swap(x, axis, size, key):
    return lax.ppermute(x, axis, [(at, at ^ key) for at in range(size)])


def chip_blocks(own, row, beside, pairs):
    per = own.shape[1]
    arrays, tables = [own], []
    operators = [(0, op, op, 0) for op in range(per)]
    if pairs == 8:
        for key in (2, 4):
            operators += [(len(arrays), op, op, key) for op in range(per)]
            arrays.append(swap(own, "pair", pairs, key))
        operators += [(3, op, op, 6) for op in range(per)]
        arrays += [
            swap(pack(arrays[1], [row, beside]), "pair", pairs, 4),
            row,
            beside,
        ]
        tables = [(4, None), (5, None), (3, 0), (3, 1)]
    else:
        arrays[0] = pack(own, [row])
        tables = [(0, 0)]
        for key in range(2, pairs, 2):
            operators += [(len(arrays), op, op, key) for op in range(per)]
            tables.append((len(arrays), 0))
            arrays.append(swap(arrays[0], "pair", pairs, key))
    return arrays, operators, tables


def on_device(pairs, sec, normal_ops, integrals, site_terms, basis):
    _, norms, rows, depth = normal_ops.shape
    _, sites, _, cols = basis.shape
    comps = integrals.shape[1]
    shape = (2, comps, rows, depth)
    two = swap(normal_ops, "sec", sec, 2)
    one = swap(normal_ops, "sec", sec, 1)
    beside = swap(integrals, "pair", pairs, 2)
    sibling = swap(integrals, "pair", pairs, 1)
    basis_split, site_part, row = prepare(basis, site_terms, integrals, rows, depth)
    arrays, operators, tables = chip_blocks(normal_ops, row, beside, pairs)
    two = after(two, sibling)
    three = swap(two, "sec", sec, 1)
    two = after(after(two, one), arrays[2])
    normals = [three, one, two, normal_ops]
    held = arrays + [row, sibling]
    here = [(len(arrays), None), (len(arrays) + 1, None)]
    mine, other = combine(held, operators, here, norms, shape)
    held = [two, swap(two, "pair", pairs, 1)] + arrays
    operators = [(key, op, op, key) for key in range(2) for op in range(norms)]
    tables = [(2 + at, part) for at, part in tables]
    parts = combine(held, operators, tables, norms, shape)
    comp_ops = total([mine, swap(other, "pair", pairs, 1)], [parts[0]])
    far = swap(comp_ops, "sec", sec, 3)
    near = swap(comp_ops, "sec", sec, 1)
    summed = [parts[0]]
    for key in range(2, pairs, 2):
        part = parts[key // 2]
        if key < pairs - 2:
            part = after(part, comp_ops)
        if key == 2:
            part = after(part, three)
        summed.append(swap(part, "pair", pairs, key))
    shape = (2, norms, sites, rows, cols)
    early = renorm(normals, range(1, sec), basis_split, None, shape)
    new_normal = renorm(normals, range(1), basis_split, early, shape, True)
    shape = (2, comps, sites, rows, cols)
    arrived = [far, near, tuple(summed), comp_ops]
    early = renorm(arrived, range(3, sec), basis_split, site_part, shape)
    return new_normal, renorm(arrived, range(3), basis_split, early, shape, True)


def solution(mesh):
    placed = (
        P(None, "pair", None, "sec"),
        P(None, "pair", None),
        P(None, "pair", None, None),
        P(None, None, None, "sec"),
    )
    return jax.shard_map(
        functools.partial(on_device, mesh.shape["pair"], mesh.shape["sec"]),
        mesh=mesh,
        in_specs=placed,
        out_specs=(P(None, "pair", None, None, "sec"), P(None, "pair", None, None, "sec")),
        check_vma=False,
    )
```

```python
import functools

import jax
import jax.numpy as jnp
from jax import lax
from jax.experimental import pallas as pl
from jax.experimental.pallas import tpu as pltpu
from jax.sharding import PartitionSpec as P

VMEM_BYTES = 24 * 1024 * 1024
WIDE = 256
TILE = (8, 128)
VMEM = pl.BlockSpec(memory_space=pltpu.VMEM)
ANY = pl.BlockSpec(memory_space=pl.ANY)
HBM = pl.BlockSpec(memory_space=pltpu.HBM)


def call(kernel, out_shape, in_specs, flops, scratch_shapes=(), moved=4 << 20):
    return pl.pallas_call(
        kernel,
        out_shape=out_shape,
        in_specs=in_specs,
        out_specs=jax.tree.map(lambda _: VMEM, out_shape),
        scratch_shapes=scratch_shapes,
        cost_estimate=pl.CostEstimate(flops=flops, bytes_accessed=moved, transcendentals=0),
        compiler_params=pltpu.CompilerParams(vmem_limit_bytes=VMEM_BYTES),
    )


def split(x):
    high = x.astype(jnp.bfloat16)
    return high, (x - high.astype(jnp.float32)).astype(jnp.bfloat16)


def order(sec):
    return (3, 1, 2, 0) if sec == 4 else tuple(range(sec))


def prepare_kernel(depth, basis_hbm, site_hbm, integrals_ref, *refs):
    split_ref, part_ref, row_ref = refs[:3]
    scratch = refs[3:]
    row_ref[...] = integrals_ref[...]
    basis_ref, site_ref, basis_sem, site_sem = scratch
    _, sites, old, cols = basis_ref.shape
    rows = part_ref.shape[3]
    me = lax.axis_index("sec")
    site_copy = pltpu.make_async_copy(site_hbm, site_ref, site_sem)
    site_copy.start()
    copies = [
        (part, site, pltpu.make_async_copy(
            basis_hbm.at[part, site], basis_ref.at[part, site], basis_sem.at[part, site]
        ))
        for part in range(2)
        for site in range(sites)
    ]
    for _, _, copy in copies:
        copy.start()
    for part, site, copy in copies:
        copy.wait()
        for step, far in enumerate(order(old // depth)):
            start = pl.multiple_of((me ^ far) * depth, depth)
            high, low = split(basis_ref[part, site, pl.ds(start, depth), :])
            for which, value in enumerate((high, low, high)):
                at = pl.ds(((step * 3 + which) * 2 + part) * depth, depth)
                split_ref[at, pl.ds(site * cols, cols)] = value
    site_copy.wait()
    for comp in range(part_ref.shape[1]):
        for site in range(sites):
            real = imag = None
            for other in range(sites):
                sr, si = site_ref[0, comp, site, other], site_ref[1, comp, site, other]
                br, bi = basis_ref[0, other, :rows, :], basis_ref[1, other, :rows, :]
                tr, ti = sr * br - si * bi, sr * bi + si * br
                real = tr if real is None else real + tr
                imag = ti if imag is None else imag + ti
            part_ref[0, comp, site] = real
            part_ref[1, comp, site] = imag


def prepare(basis, site_terms, integrals, rows, depth):
    _, sites, old, cols = basis.shape
    comps = site_terms.shape[1]
    halves = jax.ShapeDtypeStruct((6 * old, sites * cols), jnp.bfloat16)
    part = jax.ShapeDtypeStruct((2, comps, sites, rows, cols), jnp.float32)
    return call(
        functools.partial(prepare_kernel, depth),
        (halves, part, jax.ShapeDtypeStruct(integrals.shape, integrals.dtype)),
        [HBM, HBM, VMEM],
        8 * comps * sites * sites * rows * cols,
        [
            pltpu.VMEM(basis.shape, basis.dtype),
            pltpu.SMEM(site_terms.shape, site_terms.dtype),
            pltpu.SemaphoreType.DMA((2, sites)),
            pltpu.SemaphoreType.DMA,
        ],
        4 << 20,
    )(basis, site_terms, integrals)


def pack(block, tables):
    _, per, rows, cols = block.shape

    def kernel(block_ref, *refs):
        out_ref = refs[-1]
        out_ref[:, :, :rows, :] = block_ref[...]
        out_ref[:, :, rows:, :] = jnp.zeros((2, per) + TILE, jnp.float32)
        for under, ref in enumerate(refs[:-1]):
            _, comps, norms = ref.shape
            for part in range(2):
                first = rows + part * comps
                out_ref[under, 0, first : first + comps, :norms] = ref[part]

    out = jax.ShapeDtypeStruct((2, per, rows + TILE[0], cols), block.dtype)
    return call(kernel, out, [VMEM] * (1 + len(tables)), 0)(block, *tables)


def after(x, *others):
    def kernel(x_ref, *refs):
        refs[-1][...] = x_ref[...]

    out = jax.ShapeDtypeStruct(x.shape, x.dtype)
    return call(kernel, out, [VMEM] + [ANY] * len(others), 0)(x, *others)


def renorm_kernel(steps, parts, carried, awaited, streamed, *refs):
    count = sum(parts)
    split_ref = refs[count]
    first = count + 1 + carried + awaited
    out_ref, left = refs[first : first + 2]
    out_hbm, out_ref, sems = (out_ref,) + refs[-2:] if streamed else (None, out_ref, None)
    _, ops, sites, rows, cols = out_ref.shape
    depth = refs[0].shape[-1]
    tall = ops * rows
    for step in range(len(steps)):
        first = sum(parts[:step])
        value = sum(refs[at][:, :, :rows, :] for at in range(first + 1, first + parts[step]))
        value = (refs[first][:, :, :rows, :] + value).reshape(2, tall, depth)
        (rh, rl), (ih, il) = split(value[0]), split(value[1])
        for which, (real, imag) in enumerate(((rh, ih), (rh, ih), (rl, il))):
            at = 2 * (step * 3 + which) * depth
            left[:tall, at : at + depth] = real
            left[:tall, at + depth : at + 2 * depth] = -imag
            left[tall:, at : at + depth] = imag
            left[tall:, at + depth : at + 2 * depth] = real
    deep = slice(6 * depth * steps[0], 6 * depth * (steps[-1] + 1))
    copies = []
    for first in range(0, sites * cols, WIDE):
        at = (deep, slice(first, first + WIDE))
        total = jnp.dot(left[...], split_ref[at], preferred_element_type=jnp.float32)
        some = range(first // cols, (first + WIDE) // cols)
        for part in range(2):
            for op in range(ops):
                for site in some:
                    across = slice(site * cols - first, site * cols - first + cols)
                    start = part * tall + op * rows
                    value = total[start : start + rows, across]
                    if carried:
                        value = value + refs[count + 1][part, op, site]
                    out_ref[part, op, site] = value
                if streamed:
                    piece = (part, op, pl.ds(some.start, len(some)))
                    copies.append(
                        pltpu.make_async_copy(
                            out_ref.at[piece], out_hbm.at[piece], sems.at[len(copies)]
                        )
                    )
                    copies[-1].start()
    for copy in copies:
        copy.wait()


def renorm(blocks, steps, basis, carry, shape, streamed=False, awaited=()):
    blocks = [block if isinstance(block, tuple) else (block,) for block in blocks]
    blocks = blocks[steps.start : steps.stop]
    parts = tuple(len(block) for block in blocks)
    args = sum(blocks, ()) + (basis,) + (() if carry is None else (carry,))
    _, ops, sites, rows, cols = shape
    depth = blocks[0][0].shape[-1]
    left = pltpu.VMEM((2 * ops * rows, 6 * depth * len(blocks)), jnp.bfloat16)
    pieces = 2 * ops * sites * cols // WIDE
    held = [pltpu.VMEM(shape, jnp.float32), pltpu.SemaphoreType.DMA((pieces,))]
    return pl.pallas_call(
        functools.partial(
            renorm_kernel, steps, parts, carry is not None, len(awaited), streamed
        ),
        out_shape=jax.ShapeDtypeStruct(shape, jnp.float32),
        in_specs=[VMEM] * len(args) + [ANY] * len(awaited),
        out_specs=HBM if streamed else VMEM,
        scratch_shapes=[left] + (held if streamed else []),
        cost_estimate=pl.CostEstimate(
            flops=24 * ops * rows * depth * len(blocks) * sites * cols,
            bytes_accessed=4 << 20,
            transcendentals=0,
        ),
        compiler_params=pltpu.CompilerParams(vmem_limit_bytes=VMEM_BYTES),
    )(*args, *awaited)


def total(parts, awaited):
    def kernel(*refs):
        refs[-1][...] = sum((ref[...] for ref in refs[1 : len(parts)]), refs[0][...])

    out = jax.ShapeDtypeStruct(parts[0].shape, parts[0].dtype)
    specs = [VMEM] * len(parts) + [ANY] * len(awaited)
    return call(kernel, out, specs, out.size * len(parts))(*parts, *awaited)


def combine_kernel(operators, tables, per, *refs):
    outs = refs[len(refs) - len(tables) :]
    comps, rows, _ = outs[0].shape[1:]
    me = lax.axis_index("pair")
    for (held, under), out_ref in zip(tables, outs):
        lane = lax.broadcasted_iota(jnp.int32, (1, refs[held].shape[-1]), 1)
        for comp in range(comps):
            real = imag = None
            for array, place, op, key in operators:
                coefficients = []
                for part in range(2):
                    at = part * comps + comp
                    if under is None:
                        row = refs[held][part, comp : comp + 1, :]
                    else:
                        row = refs[held][under, 0, rows + at : rows + at + 1, :]
                    here = jnp.where(lane == (me ^ key) * per + op, row, 0.0)
                    coefficients.append(jnp.sum(here, axis=1, keepdims=True))
                cr, ci = coefficients
                br, bi = (refs[array][part, place, :rows, :] for part in range(2))
                tr, ti = cr * br - ci * bi, cr * bi + ci * br
                real = tr if real is None else real + tr
                imag = ti if imag is None else imag + ti
            out_ref[0, comp] = real
            out_ref[1, comp] = imag


def combine(arrays, operators, tables, per, shape, awaited=()):
    rows, cols = shape[2:]
    return call(
        functools.partial(combine_kernel, operators, tables, per),
        (jax.ShapeDtypeStruct(shape, jnp.float32),) * len(tables),
        [VMEM] * len(arrays) + [ANY] * len(awaited),
        8 * len(tables) * len(operators) * rows * cols,
        moved=4 << 20,
    )(*arrays, *awaited)


def swap(x, axis, size, key):
    return lax.ppermute(x, axis, [(at, at ^ key) for at in range(size)])


def chip_blocks(own, row, beside, pairs):
    per = own.shape[1]
    arrays, tables = [own], []
    operators = [(0, op, op, 0) for op in range(per)]
    if pairs == 8:
        for key in (2, 4):
            operators += [(len(arrays), op, op, key) for op in range(per)]
            arrays.append(swap(own, "pair", pairs, key))
        operators += [(3, op, op, 6) for op in range(per)]
        arrays += [
            swap(pack(arrays[1], [row, beside]), "pair", pairs, 4),
            row,
            beside,
        ]
        tables = [(4, None), (5, None), (3, 0), (3, 1)]
    else:
        arrays[0] = pack(own, [row])
        tables = [(0, 0)]
        for key in range(2, pairs, 2):
            operators += [(len(arrays), op, op, key) for op in range(per)]
            tables.append((len(arrays), 0))
            arrays.append(swap(arrays[0], "pair", pairs, key))
    return arrays, operators, tables


def on_device(pairs, sec, normal_ops, integrals, site_terms, basis):
    _, norms, rows, depth = normal_ops.shape
    _, sites, _, cols = basis.shape
    comps = integrals.shape[1]
    shape = (2, comps, rows, depth)
    two = swap(normal_ops, "sec", sec, 2)
    one = swap(normal_ops, "sec", sec, 1)
    beside = swap(integrals, "pair", pairs, 2)
    sibling = swap(integrals, "pair", pairs, 1)
    basis_split, site_part, row = prepare(basis, site_terms, integrals, rows, depth)
    arrays, operators, tables = chip_blocks(normal_ops, row, beside, pairs)
    two = after(two, sibling)
    three = swap(two, "sec", sec, 1)
    two = after(after(two, one), arrays[2])
    normals = [three, one, two, normal_ops]
    held = arrays + [row, sibling]
    here = [(len(arrays), None), (len(arrays) + 1, None)]
    mine, other = combine(held, operators, here, norms, shape)
    held = [two, swap(two, "pair", pairs, 1)] + arrays
    operators = [(key, op, op, key) for key in range(2) for op in range(norms)]
    tables = [(2 + at, part) for at, part in tables]
    parts = combine(held, operators, tables, norms, shape)
    comp_ops = total([mine, swap(other, "pair", pairs, 1)], [parts[0]])
    far = swap(comp_ops, "sec", sec, 3)
    near = swap(comp_ops, "sec", sec, 1)
    summed = [parts[0]]
    for key in range(2, pairs, 2):
        part = parts[key // 2]
        if key == 2:
            part = after(part, comp_ops)
        if key == 2:
            part = after(part, three)
        summed.append(swap(part, "pair", pairs, key))
    shape = (2, norms, sites, rows, cols)
    early = renorm(normals, range(1, sec), basis_split, None, shape)
    new_normal = renorm(normals, range(1), basis_split, early, shape, True)
    shape = (2, comps, sites, rows, cols)
    arrived = [far, near, tuple(summed), comp_ops]
    early = renorm(arrived, range(3, sec), basis_split, site_part, shape)
    return new_normal, renorm(arrived, range(3), basis_split, early, shape, True)


def solution(mesh):
    placed = (
        P(None, "pair", None, "sec"),
        P(None, "pair", None),
        P(None, "pair", None, None),
        P(None, None, None, "sec"),
    )
    return jax.shard_map(
        functools.partial(on_device, mesh.shape["pair"], mesh.shape["sec"]),
        mesh=mesh,
        in_specs=placed,
        out_specs=(P(None, "pair", None, None, "sec"), P(None, "pair", None, None, "sec")),
        check_vma=False,
    )
```

```python
import functools

import jax
import jax.numpy as jnp
from jax import lax
from jax.experimental import pallas as pl
from jax.experimental.pallas import tpu as pltpu
from jax.sharding import PartitionSpec as P

VMEM_BYTES = 24 * 1024 * 1024
WIDE = 256
TILE = (8, 128)
VMEM = pl.BlockSpec(memory_space=pltpu.VMEM)
ANY = pl.BlockSpec(memory_space=pl.ANY)
HBM = pl.BlockSpec(memory_space=pltpu.HBM)


def call(kernel, out_shape, in_specs, flops, scratch_shapes=(), moved=4 << 20):
    return pl.pallas_call(
        kernel,
        out_shape=out_shape,
        in_specs=in_specs,
        out_specs=jax.tree.map(lambda _: VMEM, out_shape),
        scratch_shapes=scratch_shapes,
        cost_estimate=pl.CostEstimate(flops=flops, bytes_accessed=moved, transcendentals=0),
        compiler_params=pltpu.CompilerParams(vmem_limit_bytes=VMEM_BYTES),
    )


def split(x):
    high = x.astype(jnp.bfloat16)
    return high, (x - high.astype(jnp.float32)).astype(jnp.bfloat16)


def order(sec):
    return (3, 2, 1, 0) if sec == 4 else tuple(range(sec))


def prepare_kernel(depth, basis_hbm, site_hbm, integrals_ref, *refs):
    split_ref, part_ref, row_ref = refs[:3]
    scratch = refs[3:]
    row_ref[...] = integrals_ref[...]
    basis_ref, site_ref, basis_sem, site_sem = scratch
    _, sites, old, cols = basis_ref.shape
    rows = part_ref.shape[3]
    me = lax.axis_index("sec")
    site_copy = pltpu.make_async_copy(site_hbm, site_ref, site_sem)
    site_copy.start()
    copies = [
        (part, site, pltpu.make_async_copy(
            basis_hbm.at[part, site], basis_ref.at[part, site], basis_sem.at[part, site]
        ))
        for part in range(2)
        for site in range(sites)
    ]
    for _, _, copy in copies:
        copy.start()
    for part, site, copy in copies:
        copy.wait()
        for step, far in enumerate(order(old // depth)):
            start = pl.multiple_of((me ^ far) * depth, depth)
            high, low = split(basis_ref[part, site, pl.ds(start, depth), :])
            for which, value in enumerate((high, low, high)):
                at = pl.ds(((step * 3 + which) * 2 + part) * depth, depth)
                split_ref[at, pl.ds(site * cols, cols)] = value
    site_copy.wait()
    for comp in range(part_ref.shape[1]):
        for site in range(sites):
            real = imag = None
            for other in range(sites):
                sr, si = site_ref[0, comp, site, other], site_ref[1, comp, site, other]
                br, bi = basis_ref[0, other, :rows, :], basis_ref[1, other, :rows, :]
                tr, ti = sr * br - si * bi, sr * bi + si * br
                real = tr if real is None else real + tr
                imag = ti if imag is None else imag + ti
            part_ref[0, comp, site] = real
            part_ref[1, comp, site] = imag


def prepare(basis, site_terms, integrals, rows, depth):
    _, sites, old, cols = basis.shape
    comps = site_terms.shape[1]
    halves = jax.ShapeDtypeStruct((6 * old, sites * cols), jnp.bfloat16)
    part = jax.ShapeDtypeStruct((2, comps, sites, rows, cols), jnp.float32)
    return call(
        functools.partial(prepare_kernel, depth),
        (halves, part, jax.ShapeDtypeStruct(integrals.shape, integrals.dtype)),
        [HBM, HBM, VMEM],
        8 * comps * sites * sites * rows * cols,
        [
            pltpu.VMEM(basis.shape, basis.dtype),
            pltpu.SMEM(site_terms.shape, site_terms.dtype),
            pltpu.SemaphoreType.DMA((2, sites)),
            pltpu.SemaphoreType.DMA,
        ],
        4 << 20,
    )(basis, site_terms, integrals)


def pack(block, tables):
    _, per, rows, cols = block.shape

    def kernel(block_ref, *refs):
        out_ref = refs[-1]
        out_ref[:, :, :rows, :] = block_ref[...]
        out_ref[:, :, rows:, :] = jnp.zeros((2, per) + TILE, jnp.float32)
        for under, ref in enumerate(refs[:-1]):
            _, comps, norms = ref.shape
            for part in range(2):
                first = rows + part * comps
                out_ref[under, 0, first : first + comps, :norms] = ref[part]

    out = jax.ShapeDtypeStruct((2, per, rows + TILE[0], cols), block.dtype)
    return call(kernel, out, [VMEM] * (1 + len(tables)), 0)(block, *tables)


def after(x, *others):
    def kernel(x_ref, *refs):
        refs[-1][...] = x_ref[...]

    out = jax.ShapeDtypeStruct(x.shape, x.dtype)
    return call(kernel, out, [VMEM] + [ANY] * len(others), 0)(x, *others)


def renorm_kernel(steps, parts, carried, awaited, streamed, *refs):
    count = sum(parts)
    split_ref = refs[count]
    first = count + 1 + carried + awaited
    out_ref, left = refs[first : first + 2]
    out_hbm, out_ref, sems = (out_ref,) + refs[-2:] if streamed else (None, out_ref, None)
    _, ops, sites, rows, cols = out_ref.shape
    depth = refs[0].shape[-1]
    tall = ops * rows
    for step in range(len(steps)):
        first = sum(parts[:step])
        value = sum(refs[at][:, :, :rows, :] for at in range(first + 1, first + parts[step]))
        value = (refs[first][:, :, :rows, :] + value).reshape(2, tall, depth)
        (rh, rl), (ih, il) = split(value[0]), split(value[1])
        for which, (real, imag) in enumerate(((rh, ih), (rh, ih), (rl, il))):
            at = 2 * (step * 3 + which) * depth
            left[:tall, at : at + depth] = real
            left[:tall, at + depth : at + 2 * depth] = -imag
            left[tall:, at : at + depth] = imag
            left[tall:, at + depth : at + 2 * depth] = real
    deep = slice(6 * depth * steps[0], 6 * depth * (steps[-1] + 1))
    copies = []
    for first in range(0, sites * cols, WIDE):
        at = (deep, slice(first, first + WIDE))
        total = jnp.dot(left[...], split_ref[at], preferred_element_type=jnp.float32)
        some = range(first // cols, (first + WIDE) // cols)
        for part in range(2):
            for op in range(ops):
                for site in some:
                    across = slice(site * cols - first, site * cols - first + cols)
                    start = part * tall + op * rows
                    value = total[start : start + rows, across]
                    if carried:
                        value = value + refs[count + 1][part, op, site]
                    out_ref[part, op, site] = value
                if streamed:
                    piece = (part, op, pl.ds(some.start, len(some)))
                    copies.append(
                        pltpu.make_async_copy(
                            out_ref.at[piece], out_hbm.at[piece], sems.at[len(copies)]
                        )
                    )
                    copies[-1].start()
    for copy in copies:
        copy.wait()


def renorm(blocks, steps, basis, carry, shape, streamed=False, awaited=()):
    blocks = [block if isinstance(block, tuple) else (block,) for block in blocks]
    blocks = blocks[steps.start : steps.stop]
    parts = tuple(len(block) for block in blocks)
    args = sum(blocks, ()) + (basis,) + (() if carry is None else (carry,))
    _, ops, sites, rows, cols = shape
    depth = blocks[0][0].shape[-1]
    left = pltpu.VMEM((2 * ops * rows, 6 * depth * len(blocks)), jnp.bfloat16)
    pieces = 2 * ops * sites * cols // WIDE
    held = [pltpu.VMEM(shape, jnp.float32), pltpu.SemaphoreType.DMA((pieces,))]
    return pl.pallas_call(
        functools.partial(
            renorm_kernel, steps, parts, carry is not None, len(awaited), streamed
        ),
        out_shape=jax.ShapeDtypeStruct(shape, jnp.float32),
        in_specs=[VMEM] * len(args) + [ANY] * len(awaited),
        out_specs=HBM if streamed else VMEM,
        scratch_shapes=[left] + (held if streamed else []),
        cost_estimate=pl.CostEstimate(
            flops=24 * ops * rows * depth * len(blocks) * sites * cols,
            bytes_accessed=4 << 20,
            transcendentals=0,
        ),
        compiler_params=pltpu.CompilerParams(vmem_limit_bytes=VMEM_BYTES),
    )(*args, *awaited)


def total(parts, awaited):
    def kernel(*refs):
        refs[-1][...] = sum((ref[...] for ref in refs[1 : len(parts)]), refs[0][...])

    out = jax.ShapeDtypeStruct(parts[0].shape, parts[0].dtype)
    specs = [VMEM] * len(parts) + [ANY] * len(awaited)
    return call(kernel, out, specs, out.size * len(parts))(*parts, *awaited)


def combine_kernel(operators, tables, per, *refs):
    outs = refs[len(refs) - len(tables) :]
    comps, rows, _ = outs[0].shape[1:]
    me = lax.axis_index("pair")
    for (held, under), out_ref in zip(tables, outs):
        lane = lax.broadcasted_iota(jnp.int32, (1, refs[held].shape[-1]), 1)
        for comp in range(comps):
            real = imag = None
            for array, place, op, key in operators:
                coefficients = []
                for part in range(2):
                    at = part * comps + comp
                    if under is None:
                        row = refs[held][part, comp : comp + 1, :]
                    else:
                        row = refs[held][under, 0, rows + at : rows + at + 1, :]
                    here = jnp.where(lane == (me ^ key) * per + op, row, 0.0)
                    coefficients.append(jnp.sum(here, axis=1, keepdims=True))
                cr, ci = coefficients
                br, bi = (refs[array][part, place, :rows, :] for part in range(2))
                tr, ti = cr * br - ci * bi, cr * bi + ci * br
                real = tr if real is None else real + tr
                imag = ti if imag is None else imag + ti
            out_ref[0, comp] = real
            out_ref[1, comp] = imag


def combine(arrays, operators, tables, per, shape, awaited=()):
    rows, cols = shape[2:]
    return call(
        functools.partial(combine_kernel, operators, tables, per),
        (jax.ShapeDtypeStruct(shape, jnp.float32),) * len(tables),
        [VMEM] * len(arrays) + [ANY] * len(awaited),
        8 * len(tables) * len(operators) * rows * cols,
        moved=4 << 20,
    )(*arrays, *awaited)


def swap(x, axis, size, key):
    return lax.ppermute(x, axis, [(at, at ^ key) for at in range(size)])


def chip_blocks(own, row, beside, pairs):
    per = own.shape[1]
    arrays, tables = [own], []
    operators = [(0, op, op, 0) for op in range(per)]
    if pairs == 8:
        for key in (2, 4):
            operators += [(len(arrays), op, op, key) for op in range(per)]
            arrays.append(swap(own, "pair", pairs, key))
        operators += [(3, op, op, 6) for op in range(per)]
        arrays += [
            swap(pack(arrays[1], [row, beside]), "pair", pairs, 4),
            row,
            beside,
        ]
        tables = [(4, None), (5, None), (3, 0), (3, 1)]
    else:
        arrays[0] = pack(own, [row])
        tables = [(0, 0)]
        for key in range(2, pairs, 2):
            operators += [(len(arrays), op, op, key) for op in range(per)]
            tables.append((len(arrays), 0))
            arrays.append(swap(arrays[0], "pair", pairs, key))
    return arrays, operators, tables


def on_device(pairs, sec, normal_ops, integrals, site_terms, basis):
    _, norms, rows, depth = normal_ops.shape
    _, sites, _, cols = basis.shape
    comps = integrals.shape[1]
    shape = (2, comps, rows, depth)
    two = swap(normal_ops, "sec", sec, 2)
    one = swap(normal_ops, "sec", sec, 1)
    beside = swap(integrals, "pair", pairs, 2)
    sibling = swap(integrals, "pair", pairs, 1)
    basis_split, site_part, row = prepare(basis, site_terms, integrals, rows, depth)
    arrays, operators, tables = chip_blocks(normal_ops, row, beside, pairs)
    two = after(two, sibling)
    three = swap(two, "sec", sec, 1)
    two = after(after(two, one), arrays[2])
    normals = [three, two, one, normal_ops]
    held = arrays + [row, sibling]
    here = [(len(arrays), None), (len(arrays) + 1, None)]
    mine, other = combine(held, operators, here, norms, shape)
    held = [two, swap(two, "pair", pairs, 1)] + arrays
    operators = [(key, op, op, key) for key in range(2) for op in range(norms)]
    tables = [(2 + at, part) for at, part in tables]
    parts = combine(held, operators, tables, norms, shape)
    comp_ops = total([mine, swap(other, "pair", pairs, 1)], [parts[0]])
    far = swap(comp_ops, "sec", sec, 3)
    near = swap(comp_ops, "sec", sec, 1)
    summed = [parts[0]]
    for key in range(2, pairs, 2):
        part = parts[key // 2]
        if key == 2:
            part = after(part, comp_ops)
        if key == 2:
            part = after(part, three)
        summed.append(swap(part, "pair", pairs, key))
    shape = (2, norms, sites, rows, cols)
    early = renorm(normals, range(1, sec), basis_split, None, shape)
    new_normal = renorm(normals, range(1), basis_split, early, shape, True)
    shape = (2, comps, sites, rows, cols)
    arrived = [far, tuple(summed), near, comp_ops]
    early = renorm(arrived, range(3, sec), basis_split, site_part, shape)
    early = renorm(arrived, range(2), basis_split, early, shape)
    return new_normal, renorm(arrived, range(2, 3), basis_split, early, shape, True)


def solution(mesh):
    placed = (
        P(None, "pair", None, "sec"),
        P(None, "pair", None),
        P(None, "pair", None, None),
        P(None, None, None, "sec"),
    )
    return jax.shard_map(
        functools.partial(on_device, mesh.shape["pair"], mesh.shape["sec"]),
        mesh=mesh,
        in_specs=placed,
        out_specs=(P(None, "pair", None, None, "sec"), P(None, "pair", None, None, "sec")),
        check_vma=False,
    )
```
